512 devices in a mesh: gx: 16 (over y_hi, x, core), gy: 32 (over y_lo, z).
Axes of the slice: x: 4, y: 4 (y_hi: 2, y_lo: 2; y = y_hi * 2 + y_lo), z: 16, core: 2. Of those that a mesh axis runs over, the one named last changes fastest.
Arguments:
- weights: float32 [16, 32, 2048, 128], P('gx', 'gy'), may hold values from -1.8 to 1.8
- angles: bfloat16 [4, 16, 32, 2048, 128], P(None, 'gx', 'gy'), may hold values from -3.140625 to 3.140625
Outputs:
- transformed: float32 [16, 32, 2048, 128], P('gx', 'gy')
The draws below stay inside these ranges and needn't reach their ends.
All inputs are finite; a program needn't handle non-finite values.
Results may differ from the reference program's by a relative error of at most 0.0003.
Values sent between devices are 32-bit elements; how exact they have to be, the bound alone decides.
No kernel may reach another device: no remote copies, remote signals or barrier semaphores. Data moves between devices by JAX's collectives and lax.ppermute only.
A program may use at most 128 MiB of HBM per device.

```python
import jax
import jax.numpy as jnp
import numpy as np
from jax import lax

P_SIZE = 8
CH = 128
BOXES = 2048
LEVELS = 4
N_GX = 16
N_GY = 32


def steps_of(stream_key, shape, cuts, low, top_value):
    factor_of = 1.0
    for axis_at, parts in cuts:
        draws = jax.random.uniform(jax.random.fold_in(jax.random.fold_in(stream_key, 6), axis_at), (parts,), jnp.float32, low / len(cuts), top_value / len(cuts))
        factor_of = factor_of * jnp.repeat(jnp.exp(draws), shape[axis_at] // parts).reshape((-1,) + (1,) * (len(shape) - 1 - axis_at))
    return factor_of


def scatter_about(stream_key, dims, deviation, most, split=(), kind=jnp.bfloat16):
    values = deviation * jax.random.normal(stream_key, dims, jnp.float32)
    if split:
        values = values * steps_of(stream_key, dims, split, -0.22, 0.18)
    return jnp.clip(values, -most, most).astype(kind)


def setup_inputs(seed: int = 0) -> dict:
    key_of = jax.random.split(jax.random.key(seed), 3)
    weights = scatter_about(key_of[0], (N_GX, N_GY, BOXES, CH), 0.3, 1.8, ((0, 16), (1, 32)), jnp.float32)
    angles = jnp.clip(jax.random.uniform(key_of[1], (LEVELS, N_GX, N_GY, BOXES, CH), jnp.float32, -3.140625, 3.140625), -3.140625, 3.140625).astype(jnp.bfloat16)
    return dict(weights=weights, angles=angles)


def child_tables(degree_count):
    cheb_nodes = np.cos((2.0 * np.arange(degree_count) + 1.0) * np.pi / (2.0 * degree_count))
    lagrange = np.ones((2, degree_count, degree_count))
    for parity in range(2):
        points = (cheb_nodes + (2.0 * parity - 1.0)) / 2.0
        for target in range(degree_count):
            for source in range(degree_count):
                for others in range(degree_count):
                    if others != source:
                        lagrange[parity, target, source] *= (points[target] - cheb_nodes[others]) / (cheb_nodes[source] - cheb_nodes[others])
    return lagrange


def level_plan(count_x, count_y):
    bits_x = count_x.bit_length() - 1
    bits_y = count_y.bit_length() - 1
    return [(0, bits_x - 1), (1, bits_y - 1), (0, bits_x - 2), (1, bits_y - 2)]


def interpolate(blocks, lagrange, grid_axis):
    shaped = blocks.reshape(blocks.shape[:-1] + (2, P_SIZE, P_SIZE))
    if grid_axis == 0:
        spread = jnp.einsum('ats,...qsy->...aqty', lagrange, shaped, precision=lax.Precision.HIGHEST)
    else:
        spread = jnp.einsum('ats,...qxs->...aqxt', lagrange, shaped, precision=lax.Precision.HIGHEST)
    return spread.reshape(blocks.shape[:-1] + (2, 2 * P_SIZE * P_SIZE))


def rotate(payload, cosine, sine_part):
    square = P_SIZE * P_SIZE
    real_part = payload[..., :square]
    imag_part = payload[..., square:]
    return jnp.concatenate([cosine * real_part - sine_part * imag_part, sine_part * real_part + cosine * imag_part], axis=-1)


def one_level(weights_now, angle_now, grid_axis, bit_num, lagrange):
    brought = jnp.moveaxis(weights_now, grid_axis, 0)
    group_count = brought.shape[0]
    outer = brought.shape[1]
    low_span = 2 ** bit_num
    blocks = brought.reshape(group_count // (2 * low_span), 2, low_span, outer, 2, BOXES // 2, 2 * P_SIZE * P_SIZE)
    blocks = jnp.swapaxes(blocks, 1, 4)
    angle_now = jnp.moveaxis(angle_now, grid_axis, 0).astype(jnp.float32)
    angle_now = angle_now.reshape(group_count // (2 * low_span), 2, low_span, outer, BOXES, 2, P_SIZE * P_SIZE)
    cosine = jnp.cos(angle_now)
    sine_part = jnp.sin(angle_now)
    result = jnp.zeros(cosine.shape[:5] + (2 * P_SIZE * P_SIZE,), jnp.float32)
    for parity in range(2):
        spread = interpolate(blocks[:, :, :, :, parity], lagrange, grid_axis)
        spread = spread.reshape(spread.shape[:4] + (BOXES, 2 * P_SIZE * P_SIZE))
        result = result + rotate(spread, cosine[..., parity, :], sine_part[..., parity, :])
    result = result.reshape(group_count, outer, BOXES, 2 * P_SIZE * P_SIZE)
    return jnp.moveaxis(result, 0, grid_axis)


def reference(weights, angles):
    lagrange = jnp.asarray(child_tables(P_SIZE), jnp.float32)
    plan = level_plan(N_GX, N_GY)
    weights_now = weights
    for level_num in range(LEVELS):
        grid_axis, bit_num = plan[level_num]
        weights_now = one_level(weights_now, angles[level_num], grid_axis, bit_num, lagrange)
    return weights_now
```

```python
import functools

import jax
import jax.numpy as jnp
import ml_dtypes
import numpy as np
from jax import lax
from jax.experimental import pallas as pl
from jax.experimental.pallas import tpu as pltpu
from jax.sharding import PartitionSpec as P

P_SIZE = 8
SQUARE = P_SIZE * P_SIZE
CH = 2 * SQUARE

def half_angle_polys():
    nodes = np.cos((2 * np.arange(64) + 1) * np.pi / 128)
    top = 3.15**2
    u = (nodes + 1) / 2 * top
    x = np.sqrt(u)
    fit = np.polynomial.chebyshev.Chebyshev.fit
    power = np.polynomial.Polynomial
    sine = fit(u, np.sin(x / 2) / x, 5, domain=[0, top]).convert(kind=power)
    cosine = fit(u, 2 * np.cos(x / 2), 6, domain=[0, top]).convert(kind=power)
    return [float(v) for v in sine.coef], [float(v) for v in cosine.coef]


SINE, COSINE = half_angle_polys()


def horner(coef, u):
    total = jnp.full_like(u, coef[-1])
    for c in coef[-2::-1]:
        total = total * u + c
    return total


def cos_sin(x):
    u = x * x
    s = x * horner(SINE, u)
    c2 = horner(COSINE, u)
    return 1.0 - 2.0 * (s * s), s * c2


def child_tables(degree_count):
    cheb_nodes = np.cos((2.0 * np.arange(degree_count) + 1.0) * np.pi / (2.0 * degree_count))
    lagrange = np.ones((2, degree_count, degree_count))
    for parity in range(2):
        points = (cheb_nodes + (2.0 * parity - 1.0)) / 2.0
        for target in range(degree_count):
            for source in range(degree_count):
                for others in range(degree_count):
                    if others != source:
                        lagrange[parity, target, source] *= (
                            points[target] - cheb_nodes[others]
                        ) / (cheb_nodes[source] - cheb_nodes[others])
    return lagrange


def spread_tables(grid_axis):
    lagrange = child_tables(P_SIZE).astype(np.float32)
    table = np.zeros((2, 2, 2, SQUARE, 2, 2, 2, SQUARE), np.float32)
    for a in range(2):
        if grid_axis == 0:
            inner = np.kron(lagrange[a].T, np.eye(P_SIZE, dtype=np.float32))
        else:
            inner = np.kron(np.eye(P_SIZE, dtype=np.float32), lagrange[a].T)
        for h in range(2):
            for slot in range(2):
                for part in range(2):
                    table[h, slot, part, :, a, part, slot ^ h, :] = inner
    table = table.reshape(2, 2 * CH, 4 * CH)
    high = table.astype(ml_dtypes.bfloat16)
    low = (table - high.astype(np.float32)).astype(ml_dtypes.bfloat16)
    return high, low


def level_kernel(tile, scal, own, arr, ang, high, low, out, scratch):
    rows = own.shape[0]
    lane = lax.broadcasted_iota(jnp.int32, (tile, CH), 1)
    left = lane < SQUARE

    def one(i):
        base = i * tile
        x = jnp.concatenate([own[pl.ds(base, tile), :], arr[pl.ds(base, tile), :]], axis=1)
        x_hi = x.astype(jnp.bfloat16)
        x_lo = (x - x_hi.astype(jnp.float32)).astype(jnp.bfloat16)
        dot = functools.partial(jnp.dot, preferred_element_type=jnp.float32)
        y = dot(x_hi, high[...]) + (dot(x_lo, high[...]) + dot(x_hi, low[...]))
        scratch[...] = ang[pl.ds(2 * base, 2 * tile), :].astype(jnp.float32)
        for a in range(2):
            c, s = cos_sin(scratch[pl.ds(a, tile, stride=2), :])
            re = y[:, 2 * a * CH : (2 * a + 1) * CH]
            im = y[:, (2 * a + 1) * CH : (2 * a + 2) * CH]
            u = c * re - s * im
            v = s * re + c * im
            mixed = jnp.where(left, u, v) + pltpu.roll(jnp.where(left, v, u), SQUARE, 1)
            out[pl.ds(2 * base + a, tile, stride=2), :] = mixed

    if rows == tile:
        one(0)
    else:
        pl.loop(0, rows // tile)(lambda i: one(pl.multiple_of(i, 1)))


def level_call(scal, own, own_spec, arr, arr_spec, ang, ang_spec, tables, out_shape, out_spec, grid):
    rows = own_spec[0][-2]
    tile = min(rows, 128)
    side = lambda g, sc: (sc[0], 0, 0)
    total = 1
    for n in out_shape:
        total *= n
    return pl.pallas_call(
        functools.partial(level_kernel, tile),
        out_shape=jax.ShapeDtypeStruct(out_shape, jnp.float32),
        grid_spec=pltpu.PrefetchScalarGridSpec(
            num_scalar_prefetch=1,
            grid=(grid,),
            in_specs=[
                pl.BlockSpec(*own_spec),
                pl.BlockSpec(*arr_spec),
                pl.BlockSpec(*ang_spec),
                pl.BlockSpec((None, 2 * CH, 4 * CH), side),
                pl.BlockSpec((None, 2 * CH, 4 * CH), side),
            ],
            out_specs=pl.BlockSpec(*out_spec),
            scratch_shapes=[pltpu.VMEM((2 * tile, CH), jnp.float32)],
        ),
        compiler_params=pltpu.CompilerParams(vmem_limit_bytes=16 * 1024 * 1024),
        cost_estimate=pl.CostEstimate(
            flops=total * 4 * CH * 2 * 3, bytes_accessed=total * 4 * 3, transcendentals=0
        ),
    )(scal, own, arr, ang, *tables)


def from_partner(block, axis, bit):
    count = lax.axis_size(axis)
    route = [(low, low ^ (1 << bit)) for low in range(count)]
    return lax.ppermute(block, axis, route)


def shards(weights, angles):
    count_x, count_y = lax.axis_size("gx"), lax.axis_size("gy")
    bits_x, bits_y = count_x.bit_length() - 1, count_y.bit_length() - 1
    boxes = weights.shape[2]
    base = boxes // 16
    index_x, index_y = lax.axis_index("gx"), lax.axis_index("gy")
    h0 = index_x >> (bits_x - 1) & 1
    h1 = index_y >> (bits_y - 1) & 1
    h2 = index_x >> (bits_x - 2) & 1
    h3 = index_y >> (bits_y - 2) & 1
    tab_x = [jnp.asarray(t) for t in spread_tables(0)]
    tab_y = [jnp.asarray(t) for t in spread_tables(1)]
    w6 = weights.reshape(2, 2, 2, 2, base, CH)
    ang0 = angles.reshape(4, 2, 2, 2, 2 * base, CH)
    ang1 = angles.reshape(4, 2, 2, 4 * base, CH)
    ang2 = angles.reshape(4, 2, 8 * base, CH)
    ang3 = angles.reshape(4, 16 * base, CH)

    def pack(*values):
        return jnp.stack([jnp.asarray(v, jnp.int32) for v in values])

    def first(chunk, sel):
        at, n = chunk
        z = jnp.int32(0)
        taken = lax.dynamic_slice(
            w6, (1 - h0, z, z, sel, jnp.int32(at), z), (1, 2, 2, 1, n, CH)
        )
        return from_partner(taken.reshape(2, 2, n, CH), "gx", bits_x - 1)

    def level0(chunk, sel, arr, t1):
        at, n = chunk
        k = at // n
        return level_call(
            pack(h0, t1, sel), w6,
            ((None, None, None, None, n, CH), lambda g, sc: (sc[0], sc[1], g, sc[2], k, 0)),
            arr, ((None, None, n, CH), lambda g, sc: (sc[1], g, 0, 0)),
            ang0, ((None, None, None, None, 2 * n, CH), lambda g, sc: (0, sc[1], g, sc[2], k, 0)),
            tab_x, (2, 2 * n, CH), ((None, 2 * n, CH), lambda g, sc: (g, 0, 0)), 2,
        )

    def level1(chunk, sel, own, arr, t2):
        at, n = chunk
        k = at // n
        return level_call(
            pack(h1, t2, sel), own, ((None, n, CH), lambda g, sc: (sc[1], g, 0)),
            arr, ((None, n, CH), lambda g, sc: (sc[1], g, 0)),
            ang1, ((None, None, None, 2 * n, CH), lambda g, sc: (1, sc[1], sc[2], 2 * k + g, 0)),
            tab_y, (4 * n, CH), ((2 * n, CH), lambda g, sc: (g, 0)), 2,
        )

    def level2(chunk, sel, own, arr):
        at, n = chunk
        k = at // n
        return level_call(
            pack(h2, sel), own, ((n, CH), lambda g, sc: (g, 0)),
            arr, ((n, CH), lambda g, sc: (g, 0)),
            ang2, ((None, None, 2 * n, CH), lambda g, sc: (2, sc[1], 4 * k + g, 0)),
            tab_x, (8 * n, CH), ((2 * n, CH), lambda g, sc: (g, 0)), 4,
        )

    def level3(own, arrs, n):
        arr = jnp.concatenate(arrs, axis=0)
        rows = own.shape[0]
        return level_call(
            pack(h3), own, ((n, CH), lambda g, sc: (g, 0)),
            arr, ((n, CH), lambda g, sc: (g, 0)),
            ang3, ((None, 2 * n, CH), lambda g, sc: (3, g, 0)),
            tab_y, (2 * rows, CH), ((2 * n, CH), lambda g, sc: (g, 0)), rows // n,
        )

    def through(chunk, sel):
        arr = first(chunk, sel)
        send = level0(chunk, sel, arr, 1 - h1)
        arr1 = from_partner(send, "gy", bits_y - 1)
        keep = level0(chunk, sel, arr, h1)
        send = level1(chunk, sel, keep, arr1, 1 - h2)
        arr2 = from_partner(send, "gx", bits_x - 2)
        keep = level1(chunk, sel, keep, arr1, h2)
        return level2(chunk, sel, keep, arr2)

    chunks = [(0, base // 2), (base // 2, base // 2)]
    arrived = [
        from_partner(through(chunk, 1 - h3), "gy", bits_y - 2) for chunk in chunks
    ]
    kept = through((0, base), h3)
    out = level3(kept, arrived, base)
    return out.reshape(1, 1, boxes, CH)


def solution(mesh):
    return jax.shard_map(
        shards,
        mesh=mesh,
        in_specs=(P("gx", "gy", None, None), P(None, "gx", "gy", None, None)),
        out_specs=P("gx", "gy", None, None),
        check_vma=False,
    )
```

```python
import functools

import jax
import jax.numpy as jnp
import ml_dtypes
import numpy as np
from jax import lax
from jax.experimental import pallas as pl
from jax.experimental.pallas import tpu as pltpu
from jax.sharding import PartitionSpec as P

P_SIZE = 8
SQUARE = P_SIZE * P_SIZE
CH = 2 * SQUARE

def half_angle_polys():
    nodes = np.cos((2 * np.arange(64) + 1) * np.pi / 128)
    top = 3.15**2
    u = (nodes + 1) / 2 * top
    x = np.sqrt(u)
    fit = np.polynomial.chebyshev.Chebyshev.fit
    power = np.polynomial.Polynomial
    sine = fit(u, np.sin(x / 2) / x, 5, domain=[0, top]).convert(kind=power)
    cosine = fit(u, 2 * np.cos(x / 2), 6, domain=[0, top]).convert(kind=power)
    return [float(v) for v in sine.coef], [float(v) for v in cosine.coef]


SINE, COSINE = half_angle_polys()


def horner(coef, u):
    total = jnp.full_like(u, coef[-1])
    for c in coef[-2::-1]:
        total = total * u + c
    return total


def cos_sin(x):
    u = x * x
    s = x * horner(SINE, u)
    c2 = horner(COSINE, u)
    return 1.0 - 2.0 * (s * s), s * c2


def child_tables(degree_count):
    cheb_nodes = np.cos((2.0 * np.arange(degree_count) + 1.0) * np.pi / (2.0 * degree_count))
    lagrange = np.ones((2, degree_count, degree_count))
    for parity in range(2):
        points = (cheb_nodes + (2.0 * parity - 1.0)) / 2.0
        for target in range(degree_count):
            for source in range(degree_count):
                for others in range(degree_count):
                    if others != source:
                        lagrange[parity, target, source] *= (
                            points[target] - cheb_nodes[others]
                        ) / (cheb_nodes[source] - cheb_nodes[others])
    return lagrange


def child_blocks():
    lagrange = child_tables(P_SIZE).astype(np.float32)
    eye = np.eye(P_SIZE, dtype=np.float32)
    blocks = np.zeros((2, 2, 2, SQUARE, CH), np.float32)
    for a in range(2):
        turned = lagrange[a].T
        for slot in range(2):
            half = slice(slot * SQUARE, (slot + 1) * SQUARE)
            blocks[0, a, slot, :, half] = np.kron(turned, eye)
            blocks[1, a, slot, :, half] = np.kron(eye, turned)
    return blocks.reshape(8 * SQUARE, CH)


def expand(blocks, outs):
    for out in outs:
        out[...] = jnp.zeros_like(out)
    for axis in range(2):
        for a in range(2):
            for slot in range(2):
                part = blocks[pl.ds(((axis * 2 + a) * 2 + slot) * SQUARE, SQUARE), :]
                high = part.astype(jnp.bfloat16)
                low = (part - high.astype(jnp.float32)).astype(jnp.bfloat16)
                for k in range(2):
                    rows = pl.ds(slot * CH + k * SQUARE, SQUARE)
                    columns = pl.ds((2 * a + k) * CH, CH)
                    outs[2 * axis][rows, columns] = high
                    outs[2 * axis + 1][rows, columns] = low


VMEM = pl.BlockSpec(memory_space=pltpu.VMEM)
HBM = pl.BlockSpec(memory_space=pltpu.HBM)


def limits(mib=6):
    return pltpu.CompilerParams(vmem_limit_bytes=mib * 1024 * 1024)


def load_kernel(weights, angles, blocks, near_weights, near_angles, *rest):
    sems = rest[-1]
    copies = [
        pltpu.make_async_copy(weights, near_weights, sems.at[0]),
        pltpu.make_async_copy(angles, near_angles, sems.at[1]),
    ]
    for copy in copies:
        copy.start()
    expand(blocks, rest[:-1])
    for copy in copies:
        copy.wait()


def load(weights, angles):
    part = jax.ShapeDtypeStruct((2 * CH, 4 * CH), jnp.bfloat16)
    return pl.pallas_call(
        load_kernel,
        out_shape=[
            jax.ShapeDtypeStruct(weights.shape, weights.dtype),
            jax.ShapeDtypeStruct(angles.shape, angles.dtype),
        ]
        + [part] * 4,
        in_specs=[HBM, HBM, VMEM],
        out_specs=[VMEM] * 6,
        scratch_shapes=[pltpu.SemaphoreType.DMA((2,))],
        compiler_params=limits(48),
        cost_estimate=pl.CostEstimate(
            flops=0, bytes_accessed=4 * 1024 * 1024, transcendentals=0
        ),
    )(weights, angles, jnp.asarray(child_blocks()))


def take_kernel(rows, n, weights, out, sems):
    copies = [
        pltpu.make_async_copy(
            weights.at[pl.ds(row, n)], out.at[pl.ds(k * n, n)], sems.at[k]
        )
        for k, row in enumerate(rows())
    ]
    for copy in copies:
        copy.start()
    for copy in copies:
        copy.wait()


def take(weights, rows, n, where):
    return pl.pallas_call(
        functools.partial(take_kernel, rows, n),
        out_shape=jax.ShapeDtypeStruct((4 * n, CH), jnp.float32),
        in_specs=[where],
        out_specs=VMEM,
        scratch_shapes=[pltpu.SemaphoreType.DMA((4,))],
        compiler_params=limits(48 if where is HBM else 6),
        cost_estimate=pl.CostEstimate(
            flops=0, bytes_accessed=4 * 1024 * 1024, transcendentals=0
        ),
    )(weights)


def own_bit(k):
    axis = ("gx", "gy")[k % 2]
    bit = lax.axis_size(axis).bit_length() - 2 - k // 2
    return lax.axis_index(axis) >> bit & 1


def turn(y, angle):
    c, s = cos_sin(angle)
    re, im = y[:, :CH], y[:, CH:]
    u = c * re - s * im
    v = s * re + c * im
    left = lax.broadcasted_iota(jnp.int32, u.shape, 1) < SQUARE
    return jnp.where(left, u, v) + pltpu.roll(jnp.where(left, v, u), SQUARE, 1)


def level_kernel(level, segments, tile, own, arr, ang, high, low, out, scratch):
    upper = own_bit(level) == 1

    def piece(parts):
        count = sum(n for *_, n in parts)
        near, far = (
            jnp.concatenate([ref[pl.ds(row[k], row[4]), :] for row in parts], axis=0)
            for k, ref in ((0, own), (1, arr))
        )
        x = jnp.concatenate([jnp.where(upper, far, near), jnp.where(upper, near, far)], axis=1)
        x_hi = x.astype(jnp.bfloat16)
        x_lo = (x - x_hi.astype(jnp.float32)).astype(jnp.bfloat16)
        dot = functools.partial(jnp.dot, preferred_element_type=jnp.float32)
        y = dot(x_hi, high[...]) + (dot(x_lo, high[...]) + dot(x_hi, low[...]))
        at = 0
        for _, _, row, _, n in parts:
            scratch[pl.ds(2 * at, 2 * n), :] = ang[pl.ds(row, 2 * n), :].astype(jnp.float32)
            at += n
        for a in range(2):
            turned = turn(
                y[:, 2 * a * CH : 2 * (a + 1) * CH], scratch[pl.ds(a, count, stride=2), :]
            )
            at = 0
            for _, _, _, row, n in parts:
                out[pl.ds(row + a, n, stride=2), :] = turned[at : at + n]
                at += n

    parts = segments()
    if parts[0][4] <= tile:
        piece(parts)
        return

    for row_own, row_arr, row_ang, row_out, n in parts:

        def step(i):
            b = pl.multiple_of(i * tile, tile)
            piece([(row_own + b, row_arr + b, row_ang + 2 * b, row_out + 2 * b, tile)])

        pl.loop(0, n // tile)(step)


def level_call(level, segments, own, arr, ang, table, rows):
    tile = min(rows // 2, 256)
    return pl.pallas_call(
        functools.partial(level_kernel, level, segments, tile),
        out_shape=jax.ShapeDtypeStruct((rows, CH), jnp.float32),
        in_specs=[VMEM] * 5,
        out_specs=VMEM,
        scratch_shapes=[pltpu.VMEM((2 * tile, CH), jnp.float32)],
        compiler_params=limits(),
        cost_estimate=pl.CostEstimate(
            flops=0, bytes_accessed=rows * 8 * 1024, transcendentals=0
        ),
    )(own, arr, ang, *table)


def last_kernel(own, arr, ang, high, low, *rest):
    out, scratch = rest[-2:]
    n = own.shape[0]
    level_kernel(3, lambda: [(0, 0, 0, 0, n)], n, own, arr, ang, high, low, out, scratch)


def last_call(own, arr, ang, table, row, earlier, boxes):
    rows = arr.shape[0]
    tile = min(rows, 256)
    k = row // tile
    whole = lambda g: (0, 0)
    operands = [own, arr, ang, *table]
    specs = [
        pl.BlockSpec((tile, CH), lambda g: (k + g, 0)),
        pl.BlockSpec((tile, CH), lambda g: (g, 0)),
        pl.BlockSpec((2 * tile, CH), lambda g: (3 * (boxes // 2 // tile) + k + g, 0)),
        VMEM,
        VMEM,
    ]
    aliases = {}
    if earlier is not None:
        aliases = {len(operands): 0}
        operands.append(earlier)
        specs.append(pl.BlockSpec(memory_space=pl.ANY))
    return pl.pallas_call(
        last_kernel,
        out_shape=jax.ShapeDtypeStruct((boxes, CH), jnp.float32),
        grid=(rows // tile,),
        in_specs=specs,
        out_specs=pl.BlockSpec((2 * tile, CH), lambda g: (k + g, 0)),
        scratch_shapes=[pltpu.VMEM((2 * tile, CH), jnp.float32)],
        input_output_aliases=aliases,
        compiler_params=limits(),
        cost_estimate=pl.CostEstimate(
            flops=0, bytes_accessed=rows * 16 * 1024, transcendentals=0
        ),
    )(*operands)


def from_partner(block, axis, bit):
    count = lax.axis_size(axis)
    route = [(low, low ^ (1 << bit)) for low in range(count)]
    return lax.ppermute(block, axis, route)


def after(value, *others):
    return lax.optimization_barrier((value, *others))[0]


def shards(weights, angles):
    bits_x = lax.axis_size("gx").bit_length() - 1
    bits_y = lax.axis_size("gy").bit_length() - 1
    boxes = weights.shape[2]
    base = boxes // 16
    far = weights.reshape(boxes, CH)
    w2, ang, *ready = load(far, angles.reshape(4 * boxes, CH))
    tab_x, tab_y = ready[:2], ready[2:]
    env = [ang, tab_x, tab_y, w2]
    aligned = lambda row: pl.multiple_of(row, 16)

    def target(k, other):
        return 1 - own_bit(k) if other else own_bit(k)

    def first(source, where, chunk, given):
        at, n = chunk

        def rows():
            low = [target(3, given) + 2 * t for t in range(4)]
            return [aligned(((1 - own_bit(0)) * 8 + k) * base + at) for k in low]

        return from_partner(take(source, rows, n, where), "gx", bits_x - 1)

    def level0(chunk, given, arr, send):
        at, n = chunk

        def segments():
            t1, t3 = target(1, send), target(3, given)
            parts = []
            for t2 in range(2):
                low = (t1 * 2 + t2) * 2 + t3
                parts.append(
                    (
                        aligned((own_bit(0) * 8 + low) * base + at),
                        aligned((t1 * 2 + t2) * n),
                        aligned(low * 2 * base + 2 * at),
                        t2 * 2 * n,
                        n,
                    )
                )
            return parts

        return level_call(0, segments, env[3], arr, env[0], env[1], 4 * n)

    def level1(chunk, given, own, arr, send):
        at, n = chunk

        def segments():
            t2, t3 = target(2, send), target(3, given)
            row = aligned(t2 * 2 * n)
            return [(row, row, aligned(boxes + (t2 * 2 + t3) * 4 * base + 4 * at), 0, 2 * n)]

        return level_call(1, segments, own, arr, env[0], env[2], 4 * n)

    def level2(chunk, given, own, arr):
        at, n = chunk

        def segments():
            t3 = target(3, given)
            return [(0, 0, aligned(2 * boxes + t3 * 8 * base + 8 * at), 0, 4 * n)]

        return level_call(2, segments, own, arr, env[0], env[1], 8 * n)

    def swap1(part):
        return from_partner(part, "gy", bits_y - 1)

    def swap2(part):
        return from_partner(part, "gx", bits_x - 2)

    def swap3(part):
        return from_partner(part, "gy", bits_y - 2)

    cut = base // 2
    a, b, k = (0, cut), (cut, base - cut), (0, base)
    arr_a = first(far, HBM, a, True)
    arr_b = first(w2, VMEM, b, True)
    send_a = level0(a, True, arr_a, True)
    arr1_a = swap1(send_a)
    keep_a = level0(a, True, after(arr_a, arr_b), False)
    send_b = level0(b, True, arr_b, True)
    arr1_b = swap1(send_b)
    arr2_a = swap2(level1(a, True, keep_a, after(arr1_a, send_b), True))
    arr_k = first(after(w2, send_b), VMEM, k, False)
    keep_a = level1(a, True, keep_a, after(arr1_a, arr1_b), False)
    given_a = level2(a, True, keep_a, arr2_a)
    z_a = swap3(given_a)
    here = after(lax.axis_index("gx"), given_a[0, 0]) < lax.axis_size("gx")

    def beside(w2, ang, tab_x, tab_y, arr_b, arr1_b, arr_k):
        env[:] = [ang, tab_x, tab_y, w2]
        keep_b = level0(b, True, arr_b, False)
        arr2_b = swap2(level1(b, True, keep_b, arr1_b, True))
        send_k = level0(k, False, arr_k, True)
        arr1_k = swap1(send_k)
        keep_b = level1(b, True, keep_b, arr1_b, False)
        keep_k = level0(k, False, arr_k, False)
        arr2_k = swap2(level1(k, False, keep_k, arr1_k, True))
        given_b = level2(b, True, keep_b, arr2_b)
        z_b = swap3(given_b)
        keep_k = level1(k, False, keep_k, arr1_k, False)
        return level2(k, False, keep_k, arr2_k), z_b

    def nothing(*_):
        return jnp.zeros((8 * base, CH)), jnp.zeros((8 * b[1], CH))

    kept, z_b = lax.cond(here, beside, nothing, w2, ang, tab_x, tab_y, arr_b, arr1_b, arr_k)
    out = last_call(kept, z_a, ang, tab_y, 0, None, boxes)
    out = last_call(kept, z_b, ang, tab_y, 8 * cut, out, boxes)
    return out.reshape(1, 1, boxes, CH)


def solution(mesh):
    return jax.shard_map(
        shards,
        mesh=mesh,
        in_specs=(P("gx", "gy", None, None), P(None, "gx", "gy", None, None)),
        out_specs=P("gx", "gy", None, None),
        check_vma=False,
    )
```

```python
import functools

import jax
import jax.numpy as jnp
import ml_dtypes
import numpy as np
from jax import lax
from jax.experimental import pallas as pl
from jax.experimental.pallas import tpu as pltpu
from jax.sharding import PartitionSpec as P

P_SIZE = 8
SQUARE = P_SIZE * P_SIZE
CH = 2 * SQUARE

def half_angle_polys():
    nodes = np.cos((2 * np.arange(64) + 1) * np.pi / 128)
    top = 3.15**2
    u = (nodes + 1) / 2 * top
    x = np.sqrt(u)
    fit = np.polynomial.chebyshev.Chebyshev.fit
    power = np.polynomial.Polynomial
    sine = fit(u, np.sin(x / 2) / x, 5, domain=[0, top]).convert(kind=power)
    cosine = fit(u, 2 * np.cos(x / 2), 6, domain=[0, top]).convert(kind=power)
    return [float(v) for v in sine.coef], [float(v) for v in cosine.coef]


COST_A, COST_B = 7 * 1024 * 1024, 4 * 1024 * 1024
SINE, COSINE = half_angle_polys()


def horner(coef, u):
    total = jnp.full_like(u, coef[-1])
    for c in coef[-2::-1]:
        total = total * u + c
    return total


def cos_sin(x):
    u = x * x
    s = x * horner(SINE, u)
    c2 = horner(COSINE, u)
    return 1.0 - 2.0 * (s * s), s * c2


def child_tables(degree_count):
    cheb_nodes = np.cos((2.0 * np.arange(degree_count) + 1.0) * np.pi / (2.0 * degree_count))
    lagrange = np.ones((2, degree_count, degree_count))
    for parity in range(2):
        points = (cheb_nodes + (2.0 * parity - 1.0)) / 2.0
        for target in range(degree_count):
            for source in range(degree_count):
                for others in range(degree_count):
                    if others != source:
                        lagrange[parity, target, source] *= (
                            points[target] - cheb_nodes[others]
                        ) / (cheb_nodes[source] - cheb_nodes[others])
    return lagrange


def child_blocks():
    lagrange = child_tables(P_SIZE).astype(np.float32)
    eye = np.eye(P_SIZE, dtype=np.float32)
    blocks = np.zeros((2, 2, 2, SQUARE, CH), np.float32)
    for a in range(2):
        turned = lagrange[a].T
        for slot in range(2):
            half = slice(slot * SQUARE, (slot + 1) * SQUARE)
            blocks[0, a, slot, :, half] = np.kron(turned, eye)
            blocks[1, a, slot, :, half] = np.kron(eye, turned)
    return blocks.reshape(8 * SQUARE, CH)


def expand(blocks, outs):
    for out in outs:
        out[...] = jnp.zeros_like(out)
    for axis in range(2):
        for a in range(2):
            for slot in range(2):
                part = blocks[pl.ds(((axis * 2 + a) * 2 + slot) * SQUARE, SQUARE), :]
                high = part.astype(jnp.bfloat16)
                low = (part - high.astype(jnp.float32)).astype(jnp.bfloat16)
                for k in range(2):
                    rows = pl.ds(slot * CH + k * SQUARE, SQUARE)
                    columns = pl.ds((2 * a + k) * CH, CH)
                    outs[2 * axis][rows, columns] = high
                    outs[2 * axis + 1][rows, columns] = low


VMEM = pl.BlockSpec(memory_space=pltpu.VMEM)
HBM = pl.BlockSpec(memory_space=pltpu.HBM)


def limits(mib=6):
    return pltpu.CompilerParams(vmem_limit_bytes=mib * 1024 * 1024)


def load_kernel(angles, blocks, near_angles, *rest):
    sems = rest[-1]
    copy = pltpu.make_async_copy(angles, near_angles, sems.at[0])
    copy.start()
    expand(blocks, rest[:-1])
    copy.wait()


def load(angles):
    part = jax.ShapeDtypeStruct((2 * CH, 4 * CH), jnp.bfloat16)
    return pl.pallas_call(
        load_kernel,
        out_shape=[jax.ShapeDtypeStruct(angles.shape, angles.dtype)] + [part] * 4,
        in_specs=[HBM, VMEM],
        out_specs=[VMEM] * 5,
        scratch_shapes=[pltpu.SemaphoreType.DMA((1,))],
        compiler_params=limits(48),
        cost_estimate=pl.CostEstimate(
            flops=0, bytes_accessed=4 * 1024 * 1024, transcendentals=0
        ),
    )(angles, jnp.asarray(child_blocks()))


def tables_kernel(blocks, *outs):
    expand(blocks, outs)


def make_tables(blocks):
    part = jax.ShapeDtypeStruct((2 * CH, 4 * CH), jnp.bfloat16)
    return pl.pallas_call(
        tables_kernel,
        out_shape=[part] * 4,
        in_specs=[VMEM],
        out_specs=[VMEM] * 4,
        compiler_params=limits(),
        cost_estimate=pl.CostEstimate(flops=0, bytes_accessed=1024 * 1024, transcendentals=0),
    )(blocks)


def take_kernel(rows, n, weights, out, sems):
    copies = [
        pltpu.make_async_copy(
            weights.at[pl.ds(row, n)], out.at[pl.ds(k * n, n)], sems.at[k]
        )
        for k, row in enumerate(rows())
    ]
    for copy in copies:
        copy.start()
    for copy in copies:
        copy.wait()


def take(weights, rows, n, where):
    return pl.pallas_call(
        functools.partial(take_kernel, rows, n),
        out_shape=jax.ShapeDtypeStruct((4 * n, CH), jnp.float32),
        in_specs=[where],
        out_specs=VMEM,
        scratch_shapes=[pltpu.SemaphoreType.DMA((4,))],
        compiler_params=limits(48 if where is HBM else 6),
        cost_estimate=pl.CostEstimate(
            flops=0, bytes_accessed=4 * 1024 * 1024, transcendentals=0
        ),
    )(weights)


def own_bit(k):
    axis = ("gx", "gy")[k % 2]
    bit = lax.axis_size(axis).bit_length() - 2 - k // 2
    return lax.axis_index(axis) >> bit & 1


def turn(y, angle):
    c, s = cos_sin(angle)
    re, im = y[:, :CH], y[:, CH:]
    u = c * re - s * im
    v = s * re + c * im
    left = lax.broadcasted_iota(jnp.int32, u.shape, 1) < SQUARE
    return jnp.where(left, u, v) + pltpu.roll(jnp.where(left, v, u), SQUARE, 1)


def level_kernel(level, segments, tile, own, arr, ang, high, low, out, scratch):
    upper = own_bit(level) == 1

    def piece(parts):
        count = sum(n for *_, n in parts)
        near, far = (
            jnp.concatenate([ref[pl.ds(row[k], row[4]), :] for row in parts], axis=0)
            for k, ref in ((0, own), (1, arr))
        )
        x = jnp.concatenate([jnp.where(upper, far, near), jnp.where(upper, near, far)], axis=1)
        x_hi = x.astype(jnp.bfloat16)
        x_lo = (x - x_hi.astype(jnp.float32)).astype(jnp.bfloat16)
        dot = functools.partial(jnp.dot, preferred_element_type=jnp.float32)
        y = dot(x_hi, high[...]) + (dot(x_lo, high[...]) + dot(x_hi, low[...]))
        at = 0
        for _, _, row, _, n in parts:
            scratch[pl.ds(2 * at, 2 * n), :] = ang[pl.ds(row, 2 * n), :].astype(jnp.float32)
            at += n
        for a in range(2):
            turned = turn(
                y[:, 2 * a * CH : 2 * (a + 1) * CH], scratch[pl.ds(a, count, stride=2), :]
            )
            at = 0
            for _, _, _, row, n in parts:
                out[pl.ds(row + a, n, stride=2), :] = turned[at : at + n]
                at += n

    parts = segments()
    if len(parts) > 1 or parts[0][4] == tile:
        piece(parts)
        return

    for row_own, row_arr, row_ang, row_out, n in parts:

        def step(i):
            b = pl.multiple_of(i * tile, tile)
            piece([(row_own + b, row_arr + b, row_ang + 2 * b, row_out + 2 * b, tile)])

        pl.loop(0, n // tile)(step)


def far_kernel(level, segments, tile, move, own, arr, ang, high, low, out, scratch, *rest):
    near_ang, near_high, near_low, near_own, sems = rest
    parts, copies, moved, at = segments(), [], [], 0
    for row_own, row_arr, row_ang, row_out, n in parts:
        pairs = [(ang.at[pl.ds(row_ang, 2 * n)], near_ang.at[pl.ds(2 * at, 2 * n)])]
        if move:
            pairs.append((own.at[pl.ds(row_own, n)], near_own.at[pl.ds(at, n)]))
        copies += pairs
        moved.append((at if move else row_own, row_arr, 2 * at, row_out, n))
        at += n
    copies += [(high, near_high), (low, near_low)]
    copies = [
        pltpu.make_async_copy(source, target, sems.at[i])
        for i, (source, target) in enumerate(copies)
    ]
    for copy in copies:
        copy.start()
    for copy in copies:
        copy.wait()
    level_kernel(
        level, lambda: moved, tile, near_own if move else own, arr, near_ang, near_high, near_low,
        out, scratch,
    )


def level_call(level, segments, own, arr, ang, table, rows, far=False):
    steps = -(-rows // 512)
    tile = rows // 2 // steps
    kernel = functools.partial(level_kernel, level, segments, tile)
    scratch = [pltpu.VMEM((2 * tile, CH), jnp.float32)]
    specs = [VMEM] * 5
    if far:
        move = level == 0
        kernel = functools.partial(far_kernel, level, segments, tile, move)
        scratch += [
            pltpu.VMEM((rows, CH), jnp.bfloat16),
            pltpu.VMEM((2 * CH, 4 * CH), jnp.bfloat16),
            pltpu.VMEM((2 * CH, 4 * CH), jnp.bfloat16),
            pltpu.VMEM((rows // 2, CH), jnp.float32),
            pltpu.SemaphoreType.DMA((6,)),
        ]
        anywhere = pl.BlockSpec(memory_space=pl.ANY)
        specs = [anywhere if move else VMEM, VMEM] + [anywhere] * 3
    return pl.pallas_call(
        kernel,
        out_shape=jax.ShapeDtypeStruct((rows, CH), jnp.float32),
        in_specs=specs,
        out_specs=VMEM,
        scratch_shapes=scratch,
        compiler_params=limits(),
        cost_estimate=pl.CostEstimate(
            flops=0, bytes_accessed=rows * 8 * 1024, transcendentals=0
        ),
    )(own, arr, ang, *table)


def fetch_kernel(row, far, near, sem):
    copy = pltpu.make_async_copy(far.at[pl.ds(row, near.shape[0])], near, sem)
    copy.start()
    copy.wait()


def fetch(far, row, rows):
    return pl.pallas_call(
        functools.partial(fetch_kernel, row),
        out_shape=jax.ShapeDtypeStruct((rows, CH), far.dtype),
        in_specs=[pl.BlockSpec(memory_space=pl.ANY)],
        out_specs=VMEM,
        scratch_shapes=[pltpu.SemaphoreType.DMA(())],
        compiler_params=limits(),
        cost_estimate=pl.CostEstimate(flops=0, bytes_accessed=1024 * 1024, transcendentals=0),
    )(far)


def last_kernel(row, own, arr, ang, high, low, *rest):
    out, scratch, near_out, sems = rest[-4:]
    count, rows = near_out.shape[:2]
    tile = rows // 2
    copies = []
    for i in range(count):
        at = i * tile
        part = near_out.at[i]
        segment = (row + at, at, 2 * (row + at), 0, tile)
        level_kernel(3, lambda: [segment], tile, own, arr, ang, high, low, part, scratch)
        copy = pltpu.make_async_copy(
            part, out.at[pl.ds(2 * (row + at), rows)], sems.at[i]
        )
        copy.start()
        copies.append(copy)
    for copy in copies:
        copy.wait()


def last_call(own, arr, ang, table, row, earlier, boxes, cost):
    rows = arr.shape[0]
    count = -(-rows // 256)
    tile = rows // count
    operands = [own, arr, ang, *table]
    specs = [VMEM] * 5
    aliases = {}
    if earlier is not None:
        aliases = {len(operands): 0}
        operands.append(earlier)
        specs.append(HBM)
    return pl.pallas_call(
        functools.partial(last_kernel, row),
        out_shape=jax.ShapeDtypeStruct((boxes, CH), jnp.float32),
        in_specs=specs,
        out_specs=HBM,
        scratch_shapes=[
            pltpu.VMEM((2 * tile, CH), jnp.float32),
            pltpu.VMEM((count, 2 * tile, CH), jnp.float32),
            pltpu.SemaphoreType.DMA((count,)),
        ],
        input_output_aliases=aliases,
        compiler_params=limits(),
        cost_estimate=pl.CostEstimate(
            flops=0, bytes_accessed=cost, transcendentals=0
        ),
    )(*operands)


def from_partner(block, axis, bit):
    count = lax.axis_size(axis)
    route = [(low, low ^ (1 << bit)) for low in range(count)]
    return lax.ppermute(block, axis, route)


def after(value, *others):
    return lax.optimization_barrier((value, *others))[0]


def shards(weights, angles):
    bits_x = lax.axis_size("gx").bit_length() - 1
    bits_y = lax.axis_size("gy").bit_length() - 1
    boxes = weights.shape[2]
    base = boxes // 16
    far = weights.reshape(boxes, CH)
    ang, *ready = load(angles.reshape(4 * boxes, CH))
    w2 = far
    tab_x, tab_y = ready[:2], ready[2:]
    env = [ang, tab_x, tab_y, w2, False]
    ang_far = angles.reshape(4 * boxes, CH)
    aligned = lambda row: pl.multiple_of(row, 16)

    def target(k, other):
        return 1 - own_bit(k) if other else own_bit(k)

    def first(source, where, chunk, given):
        at, n = chunk

        def rows():
            low = [target(3, given) + 2 * t for t in range(4)]
            return [aligned(((1 - own_bit(0)) * 8 + k) * base + at) for k in low]

        taken = take(source, rows, n, where)
        return taken, from_partner(taken, "gx", bits_x - 1)

    def level0(chunk, given, arr, send):
        at, n = chunk

        def segments():
            t1, t3 = target(1, send), target(3, given)
            parts = []
            for t2 in range(2):
                low = (t1 * 2 + t2) * 2 + t3
                parts.append(
                    (
                        aligned((own_bit(0) * 8 + low) * base + at),
                        aligned((t1 * 2 + t2) * n),
                        aligned(low * 2 * base + 2 * at),
                        t2 * 2 * n,
                        n,
                    )
                )
            return parts

        return level_call(0, segments, env[3], arr, env[0], env[1], 4 * n, env[4])

    def level1(chunk, given, own, arr, send):
        at, n = chunk

        def segments():
            t2, t3 = target(2, send), target(3, given)
            row = aligned(t2 * 2 * n)
            return [(row, row, aligned(boxes + (t2 * 2 + t3) * 4 * base + 4 * at), 0, 2 * n)]

        return level_call(1, segments, own, arr, env[0], env[2], 4 * n, env[4])

    def level2(chunk, given, own, arr):
        at, n = chunk

        def segments():
            t3 = target(3, given)
            return [(0, 0, aligned(2 * boxes + t3 * 8 * base + 8 * at), 0, 4 * n)]

        return level_call(2, segments, own, arr, env[0], env[1], 8 * n, env[4])

    def swap1(part):
        return from_partner(part, "gy", bits_y - 1)

    def swap2(part):
        return from_partner(part, "gx", bits_x - 2)

    def swap3(part):
        return from_partner(part, "gy", bits_y - 2)

    cut = base // 2
    a, b, k = (0, cut), (cut, base - cut), (0, base)
    arr_a = first(far, HBM, a, True)
    arr_b = first(after(w2, arr_a[0]), VMEM, b, True)
    arr_a = arr_a[1]
    arr_b = arr_b[1]
    send_a = level0(a, True, arr_a, True)
    arr1_a = swap1(send_a)
    keep_a = level0(a, True, after(arr_a, arr_b), False)
    send_b = level0(b, True, after(arr_b, send_a), True)
    arr1_b = swap1(send_b)
    send_a = level1(a, True, keep_a, after(arr1_a, send_b), True)
    arr2_a = swap2(send_a)
    keep_b = level0(b, True, after(arr_b, send_a), False)
    send_b = level1(b, True, keep_b, arr1_b, True)
    arr2_b = swap2(send_b)
    keep_b = level1(b, True, keep_b, arr1_b, False)
    keep_a = level1(a, True, keep_a, arr1_a, False)
    given_a = level2(a, True, keep_a, after(arr2_a, send_b, keep_b))
    z_a = swap3(given_a)

    given_b = level2(b, True, keep_b, arr2_b)
    z_b = swap3(given_b)

    here = after(lax.axis_index("gx"), given_b[0, 0]) < lax.axis_size("gx")

    def beside(w2, ang, blocks):
        ready = make_tables(blocks)
        env[:] = [ang, ready[:2], ready[2:], w2, False]
        arr_k = first(w2, HBM, k, False)[1]
        arr1_k = swap1(level0(k, False, arr_k, True))
        keep_k = level0(k, False, arr_k, False)
        arr2_k = swap2(level1(k, False, keep_k, arr1_k, True))
        keep_k = level1(k, False, keep_k, arr1_k, False)
        return level2(k, False, keep_k, arr2_k)

    kept = lax.cond(
        here, beside, lambda *_: jnp.zeros((8 * base, CH)), far, ang_far, jnp.asarray(child_blocks())
    )
    near_ang = fetch(after(ang_far, kept), 3 * boxes, boxes)
    kept = after(kept, near_ang)
    out = last_call(kept, z_a, near_ang, tab_y, 0, None, boxes, COST_A)
    out = last_call(kept, z_b, near_ang, tab_y, 8 * cut, out, boxes, COST_B)
    return out.reshape(1, 1, boxes, CH)


def solution(mesh):
    return jax.shard_map(
        shards,
        mesh=mesh,
        in_specs=(P("gx", "gy", None, None), P(None, "gx", "gy", None, None)),
        out_specs=P("gx", "gy", None, None),
        check_vma=False,
    )
```

```python
import functools

import jax
import jax.numpy as jnp
import ml_dtypes
import numpy as np
from jax import lax
from jax.experimental import pallas as pl
from jax.experimental.pallas import tpu as pltpu
from jax.sharding import PartitionSpec as P

P_SIZE = 8
SQUARE = P_SIZE * P_SIZE
CH = 2 * SQUARE

def half_angle_polys():
    nodes = np.cos((2 * np.arange(64) + 1) * np.pi / 128)
    top = 3.15**2
    u = (nodes + 1) / 2 * top
    x = np.sqrt(u)
    fit = np.polynomial.chebyshev.Chebyshev.fit
    power = np.polynomial.Polynomial
    sine = fit(u, np.sin(x / 2) / x, 5, domain=[0, top]).convert(kind=power)
    cosine = fit(u, 2 * np.cos(x / 2), 6, domain=[0, top]).convert(kind=power)
    return [float(v) for v in sine.coef], [float(v) for v in cosine.coef]


COST_A, COST_B = 7 * 1024 * 1024, 4 * 1024 * 1024
SINE, COSINE = half_angle_polys()


def horner(coef, u):
    total = jnp.full_like(u, coef[-1])
    for c in coef[-2::-1]:
        total = total * u + c
    return total


def cos_sin(x):
    u = x * x
    s = x * horner(SINE, u)
    c2 = horner(COSINE, u)
    return 1.0 - 2.0 * (s * s), s * c2


def child_tables(degree_count):
    cheb_nodes = np.cos((2.0 * np.arange(degree_count) + 1.0) * np.pi / (2.0 * degree_count))
    lagrange = np.ones((2, degree_count, degree_count))
    for parity in range(2):
        points = (cheb_nodes + (2.0 * parity - 1.0)) / 2.0
        for target in range(degree_count):
            for source in range(degree_count):
                for others in range(degree_count):
                    if others != source:
                        lagrange[parity, target, source] *= (
                            points[target] - cheb_nodes[others]
                        ) / (cheb_nodes[source] - cheb_nodes[others])
    return lagrange


def child_blocks():
    lagrange = child_tables(P_SIZE).astype(np.float32)
    eye = np.eye(P_SIZE, dtype=np.float32)
    blocks = np.zeros((2, 2, 2, SQUARE, CH), np.float32)
    for a in range(2):
        turned = lagrange[a].T
        for slot in range(2):
            half = slice(slot * SQUARE, (slot + 1) * SQUARE)
            blocks[0, a, slot, :, half] = np.kron(turned, eye)
            blocks[1, a, slot, :, half] = np.kron(eye, turned)
    return blocks.reshape(8 * SQUARE, CH)


def expand(blocks, outs):
    for out in outs:
        out[...] = jnp.zeros_like(out)
    for axis in range(2):
        for a in range(2):
            for slot in range(2):
                part = blocks[pl.ds(((axis * 2 + a) * 2 + slot) * SQUARE, SQUARE), :]
                high = part.astype(jnp.bfloat16)
                low = (part - high.astype(jnp.float32)).astype(jnp.bfloat16)
                for k in range(2):
                    rows = pl.ds(slot * CH + k * SQUARE, SQUARE)
                    columns = pl.ds((2 * a + k) * CH, CH)
                    outs[2 * axis][rows, columns] = high
                    outs[2 * axis + 1][rows, columns] = low


VMEM = pl.BlockSpec(memory_space=pltpu.VMEM)
HBM = pl.BlockSpec(memory_space=pltpu.HBM)


def limits(mib=6):
    return pltpu.CompilerParams(vmem_limit_bytes=mib * 1024 * 1024)


PIECES = 8


def load_kernel(angles, blocks, near_angles, *rest):
    near_blocks, sems = rest[-2:]
    first = pltpu.make_async_copy(blocks, near_blocks, sems.at[PIECES])
    first.start()
    rows = angles.shape[0] // PIECES
    copies = []
    for i in range(PIECES):
        part = pl.ds(i * rows, rows)
        copies.append(
            pltpu.make_async_copy(angles.at[part], near_angles.at[part], sems.at[i])
        )
        copies[-1].start()
    first.wait()
    expand(near_blocks, rest[:-2])
    for copy in copies:
        copy.wait()


def load(angles):
    part = jax.ShapeDtypeStruct((2 * CH, 4 * CH), jnp.bfloat16)
    blocks = jnp.asarray(child_blocks())
    return pl.pallas_call(
        load_kernel,
        out_shape=[jax.ShapeDtypeStruct(angles.shape, angles.dtype)] + [part] * 4,
        in_specs=[HBM, HBM],
        out_specs=[VMEM] * 5,
        scratch_shapes=[
            pltpu.VMEM(blocks.shape, blocks.dtype),
            pltpu.SemaphoreType.DMA((PIECES + 1,)),
        ],
        compiler_params=limits(48),
        cost_estimate=pl.CostEstimate(
            flops=0, bytes_accessed=4 * 1024 * 1024, transcendentals=0
        ),
    )(angles, blocks)


def tables_kernel(blocks, *outs):
    expand(blocks, outs)


def make_tables(blocks):
    part = jax.ShapeDtypeStruct((2 * CH, 4 * CH), jnp.bfloat16)
    return pl.pallas_call(
        tables_kernel,
        out_shape=[part] * 4,
        in_specs=[VMEM],
        out_specs=[VMEM] * 4,
        compiler_params=limits(),
        cost_estimate=pl.CostEstimate(flops=0, bytes_accessed=1024 * 1024, transcendentals=0),
    )(blocks)


def take_kernel(rows, weights, *rest):
    outs, sems = rest[:-1], rest[-1]
    copies = []
    for out, parts in zip(outs, rows()):
        at = 0
        for row, n in parts:
            copies.append(
                pltpu.make_async_copy(
                    weights.at[pl.ds(row, n)], out.at[pl.ds(at, n)], sems.at[len(copies)]
                )
            )
            at += n
    for copy in copies:
        copy.start()
    for copy in copies:
        copy.wait()


def take(weights, rows, sizes, parts):
    return pl.pallas_call(
        functools.partial(take_kernel, rows),
        out_shape=[jax.ShapeDtypeStruct((n, CH), jnp.float32) for n in sizes],
        in_specs=[HBM],
        out_specs=[VMEM] * len(sizes),
        scratch_shapes=[pltpu.SemaphoreType.DMA((parts,))],
        compiler_params=limits(48),
        cost_estimate=pl.CostEstimate(
            flops=0, bytes_accessed=20 * 1024 * 1024, transcendentals=0
        ),
    )(weights)


def own_bit(k):
    axis = ("gx", "gy")[k % 2]
    bit = lax.axis_size(axis).bit_length() - 2 - k // 2
    return lax.axis_index(axis) >> bit & 1


def turn(y, angle):
    c, s = cos_sin(angle)
    re, im = y[:, :CH], y[:, CH:]
    u = c * re - s * im
    v = s * re + c * im
    left = lax.broadcasted_iota(jnp.int32, u.shape, 1) < SQUARE
    return jnp.where(left, u, v) + pltpu.roll(jnp.where(left, v, u), SQUARE, 1)


def level_kernel(level, segments, tile, own, arr, ang, high, low, out, scratch):
    upper = own_bit(level) == 1

    def piece(parts):
        count = sum(n for *_, n in parts)
        near, far = (
            jnp.concatenate([ref[pl.ds(row[k], row[4]), :] for row in parts], axis=0)
            for k, ref in ((0, own), (1, arr))
        )
        x = jnp.concatenate([jnp.where(upper, far, near), jnp.where(upper, near, far)], axis=1)
        x_hi = x.astype(jnp.bfloat16)
        x_lo = (x - x_hi.astype(jnp.float32)).astype(jnp.bfloat16)
        dot = functools.partial(jnp.dot, preferred_element_type=jnp.float32)
        y = dot(x_hi, high[...]) + (dot(x_lo, high[...]) + dot(x_hi, low[...]))
        at = 0
        for _, _, row, _, n in parts:
            scratch[pl.ds(2 * at, 2 * n), :] = ang[pl.ds(row, 2 * n), :].astype(jnp.float32)
            at += n
        for a in range(2):
            turned = turn(
                y[:, 2 * a * CH : 2 * (a + 1) * CH], scratch[pl.ds(a, count, stride=2), :]
            )
            at = 0
            for _, _, _, row, n in parts:
                out[pl.ds(row + a, n, stride=2), :] = turned[at : at + n]
                at += n

    parts = segments()
    if len(parts) > 1 or parts[0][4] == tile:
        piece(parts)
        return

    for row_own, row_arr, row_ang, row_out, n in parts:

        def step(i):
            b = pl.multiple_of(i * tile, tile)
            piece([(row_own + b, row_arr + b, row_ang + 2 * b, row_out + 2 * b, tile)])

        pl.loop(0, n // tile)(step)


def far_kernel(level, segments, tile, move, own, arr, ang, high, low, out, scratch, *rest):
    near_ang, near_high, near_low, near_own, sems = rest
    parts, copies, moved, at = segments(), [], [], 0
    for row_own, row_arr, row_ang, row_out, n in parts:
        pairs = [(ang.at[pl.ds(row_ang, 2 * n)], near_ang.at[pl.ds(2 * at, 2 * n)])]
        if move:
            pairs.append((own.at[pl.ds(row_own, n)], near_own.at[pl.ds(at, n)]))
        copies += pairs
        moved.append((at if move else row_own, row_arr, 2 * at, row_out, n))
        at += n
    copies += [(high, near_high), (low, near_low)]
    copies = [
        pltpu.make_async_copy(source, target, sems.at[i])
        for i, (source, target) in enumerate(copies)
    ]
    for copy in copies:
        copy.start()
    for copy in copies:
        copy.wait()
    level_kernel(
        level, lambda: moved, tile, near_own if move else own, arr, near_ang, near_high, near_low,
        out, scratch,
    )


def level_call(level, segments, own, arr, ang, table, rows, far=False):
    steps = -(-rows // 512)
    tile = rows // 2 // steps
    kernel = functools.partial(level_kernel, level, segments, tile)
    scratch = [pltpu.VMEM((2 * tile, CH), jnp.float32)]
    specs = [VMEM] * 5
    if far:
        move = level == 0
        kernel = functools.partial(far_kernel, level, segments, tile, move)
        scratch += [
            pltpu.VMEM((rows, CH), jnp.bfloat16),
            pltpu.VMEM((2 * CH, 4 * CH), jnp.bfloat16),
            pltpu.VMEM((2 * CH, 4 * CH), jnp.bfloat16),
            pltpu.VMEM((rows // 2, CH), jnp.float32),
            pltpu.SemaphoreType.DMA((6,)),
        ]
        anywhere = pl.BlockSpec(memory_space=pl.ANY)
        specs = [anywhere if move else VMEM, VMEM] + [anywhere] * 3
    return pl.pallas_call(
        kernel,
        out_shape=jax.ShapeDtypeStruct((rows, CH), jnp.float32),
        in_specs=specs,
        out_specs=VMEM,
        scratch_shapes=scratch,
        compiler_params=limits(),
        cost_estimate=pl.CostEstimate(
            flops=0, bytes_accessed=rows * 8 * 1024, transcendentals=0
        ),
    )(own, arr, ang, *table)


def fetch_kernel(row, far, near, sem):
    copy = pltpu.make_async_copy(far.at[pl.ds(row, near.shape[0])], near, sem)
    copy.start()
    copy.wait()


def fetch(far, row, rows):
    return pl.pallas_call(
        functools.partial(fetch_kernel, row),
        out_shape=jax.ShapeDtypeStruct((rows, CH), far.dtype),
        in_specs=[pl.BlockSpec(memory_space=pl.ANY)],
        out_specs=VMEM,
        scratch_shapes=[pltpu.SemaphoreType.DMA(())],
        compiler_params=limits(),
        cost_estimate=pl.CostEstimate(flops=0, bytes_accessed=1024 * 1024, transcendentals=0),
    )(far)


def last_kernel(row, own, arr, ang, high, low, *rest):
    out, scratch, near_out, sems = rest[-4:]
    count, rows = near_out.shape[:2]
    tile = rows // 2
    copies = []
    for i in range(count):
        at = i * tile
        part = near_out.at[i]
        segment = (row + at, at, 2 * (row + at), 0, tile)
        level_kernel(3, lambda: [segment], tile, own, arr, ang, high, low, part, scratch)
        copy = pltpu.make_async_copy(
            part, out.at[pl.ds(2 * (row + at), rows)], sems.at[i]
        )
        copy.start()
        copies.append(copy)
    for copy in copies:
        copy.wait()


def last_call(own, arr, ang, table, row, earlier, boxes, cost):
    rows = arr.shape[0]
    count = -(-rows // 256)
    tile = rows // count
    operands = [own, arr, ang, *table]
    specs = [VMEM] * 5
    aliases = {}
    if earlier is not None:
        aliases = {len(operands): 0}
        operands.append(earlier)
        specs.append(HBM)
    return pl.pallas_call(
        functools.partial(last_kernel, row),
        out_shape=jax.ShapeDtypeStruct((boxes, CH), jnp.float32),
        in_specs=specs,
        out_specs=HBM,
        scratch_shapes=[
            pltpu.VMEM((2 * tile, CH), jnp.float32),
            pltpu.VMEM((count, 2 * tile, CH), jnp.float32),
            pltpu.SemaphoreType.DMA((count,)),
        ],
        input_output_aliases=aliases,
        compiler_params=limits(),
        cost_estimate=pl.CostEstimate(
            flops=0, bytes_accessed=cost, transcendentals=0
        ),
    )(*operands)


def from_partner(block, axis, bit):
    count = lax.axis_size(axis)
    route = [(low, low ^ (1 << bit)) for low in range(count)]
    return lax.ppermute(block, axis, route)


def after(value, *others):
    return lax.optimization_barrier((value, *others))[0]


def shards(weights, angles):
    bits_x = lax.axis_size("gx").bit_length() - 1
    bits_y = lax.axis_size("gy").bit_length() - 1
    boxes = weights.shape[2]
    base = boxes // 16
    far = weights.reshape(boxes, CH)
    ang, *ready = load(angles.reshape(4 * boxes, CH))
    w2 = far
    tab_x, tab_y = ready[:2], ready[2:]
    env = [ang, tab_x, tab_y, w2, False]
    ang_far = angles.reshape(4 * boxes, CH)
    aligned = lambda row: pl.multiple_of(row, 16)

    def target(k, other):
        return 1 - own_bit(k) if other else own_bit(k)

    def first(chunks, given):
        def rows():
            low = [target(3, given) + 2 * t for t in range(4)]
            return [
                [(aligned(((1 - own_bit(0)) * 8 + k) * base + at), n) for k in low]
                for at, n in chunks
            ]

        taken = take(far, rows, [4 * n for _, n in chunks], 4 * len(chunks))
        return [from_partner(part, "gx", bits_x - 1) for part in taken]

    def level0(chunk, given, arr, send):
        at, n = chunk

        def segments():
            t1, t3 = target(1, send), target(3, given)
            parts = []
            for t2 in range(2):
                low = (t1 * 2 + t2) * 2 + t3
                parts.append(
                    (
                        aligned((own_bit(0) * 8 + low) * base + at),
                        aligned((t1 * 2 + t2) * n),
                        aligned(low * 2 * base + 2 * at),
                        t2 * 2 * n,
                        n,
                    )
                )
            return parts

        return level_call(0, segments, env[3], arr, env[0], env[1], 4 * n, env[4])

    def level1(chunk, given, own, arr, send):
        at, n = chunk

        def segments():
            t2, t3 = target(2, send), target(3, given)
            row = aligned(t2 * 2 * n)
            return [(row, row, aligned(boxes + (t2 * 2 + t3) * 4 * base + 4 * at), 0, 2 * n)]

        return level_call(1, segments, own, arr, env[0], env[2], 4 * n, env[4])

    def level2(chunk, given, own, arr):
        at, n = chunk

        def segments():
            t3 = target(3, given)
            return [(0, 0, aligned(2 * boxes + t3 * 8 * base + 8 * at), 0, 4 * n)]

        return level_call(2, segments, own, arr, env[0], env[1], 8 * n, env[4])

    def swap1(part):
        return from_partner(part, "gy", bits_y - 1)

    def swap2(part):
        return from_partner(part, "gx", bits_x - 2)

    def swap3(part):
        return from_partner(part, "gy", bits_y - 2)

    cut = base // 2
    a, b, k = (0, cut), (cut, base - cut), (0, base)
    arr_a, arr_b = first([a, b], True)
    send_a = level0(a, True, arr_a, True)
    arr1_a = swap1(send_a)
    keep_a = level0(a, True, after(arr_a, send_a), False)
    send_b = level0(b, True, after(arr_b, keep_a), True)
    arr1_b = swap1(send_b)
    send_a = level1(a, True, keep_a, after(arr1_a, send_b), True)
    arr2_a = swap2(send_a)
    keep_b = level0(b, True, after(arr_b, send_a), False)
    send_b = level1(b, True, keep_b, arr1_b, True)
    arr2_b = swap2(send_b)
    keep_b = level1(b, True, keep_b, arr1_b, False)
    keep_a = level1(a, True, keep_a, arr1_a, False)
    given_a = level2(a, True, keep_a, after(arr2_a, send_b, keep_b))
    z_a = swap3(given_a)

    given_b = level2(b, True, keep_b, arr2_b)
    z_b = swap3(given_b)

    here = after(lax.axis_index("gx"), given_b[0, 0]) < lax.axis_size("gx")

    def beside(w2, ang, blocks):
        nonlocal far
        far = w2
        ready = make_tables(blocks)
        env[:] = [ang, ready[:2], ready[2:], w2, False]
        (arr_k,) = first([k], False)
        arr1_k = swap1(level0(k, False, arr_k, True))
        keep_k = level0(k, False, arr_k, False)
        arr2_k = swap2(level1(k, False, keep_k, arr1_k, True))
        keep_k = level1(k, False, keep_k, arr1_k, False)
        return level2(k, False, keep_k, arr2_k)

    kept = lax.cond(
        here, beside, lambda *_: jnp.zeros((8 * base, CH)), far, ang_far, jnp.asarray(child_blocks())
    )
    near_ang = fetch(after(ang_far, kept), 3 * boxes, boxes)
    kept = after(kept, near_ang)
    out = last_call(kept, z_a, near_ang, tab_y, 0, None, boxes, COST_A)
    out = last_call(kept, z_b, near_ang, tab_y, 8 * cut, out, boxes, COST_B)
    return out.reshape(1, 1, boxes, CH)


def solution(mesh):
    return jax.shard_map(
        shards,
        mesh=mesh,
        in_specs=(P("gx", "gy", None, None), P(None, "gx", "gy", None, None)),
        out_specs=P("gx", "gy", None, None),
        check_vma=False,
    )
```

```python
import functools

import jax
import jax.numpy as jnp
import ml_dtypes
import numpy as np
from jax import lax
from jax.experimental import pallas as pl
from jax.experimental.pallas import tpu as pltpu
from jax.sharding import PartitionSpec as P

P_SIZE = 8
SQUARE = P_SIZE * P_SIZE
CH = 2 * SQUARE

def half_angle_polys():
    nodes = np.cos((2 * np.arange(64) + 1) * np.pi / 128)
    top = 3.15**2
    u = (nodes + 1) / 2 * top
    x = np.sqrt(u)
    fit = np.polynomial.chebyshev.Chebyshev.fit
    power = np.polynomial.Polynomial
    sine = fit(u, np.sin(x / 2) / x, 5, domain=[0, top]).convert(kind=power)
    cosine = fit(u, 2 * np.cos(x / 2), 6, domain=[0, top]).convert(kind=power)
    return [float(v) for v in sine.coef], [float(v) for v in cosine.coef]


AHEAD = 0
SINE, COSINE = half_angle_polys()


def horner(coef, u):
    total = jnp.full_like(u, coef[-1])
    for c in coef[-2::-1]:
        total = total * u + c
    return total


def cos_sin(x):
    u = x * x
    s = x * horner(SINE, u)
    c2 = horner(COSINE, u)
    return 1.0 - 2.0 * (s * s), s * c2


def child_tables(degree_count):
    cheb_nodes = np.cos((2.0 * np.arange(degree_count) + 1.0) * np.pi / (2.0 * degree_count))
    lagrange = np.ones((2, degree_count, degree_count))
    for parity in range(2):
        points = (cheb_nodes + (2.0 * parity - 1.0)) / 2.0
        for target in range(degree_count):
            for source in range(degree_count):
                for others in range(degree_count):
                    if others != source:
                        lagrange[parity, target, source] *= (
                            points[target] - cheb_nodes[others]
                        ) / (cheb_nodes[source] - cheb_nodes[others])
    return lagrange


def child_blocks():
    lagrange = child_tables(P_SIZE).astype(np.float32)
    eye = np.eye(P_SIZE, dtype=np.float32)
    blocks = np.zeros((2, 2, 2, SQUARE, CH), np.float32)
    for a in range(2):
        turned = lagrange[a].T
        for slot in range(2):
            half = slice(slot * SQUARE, (slot + 1) * SQUARE)
            blocks[0, a, slot, :, half] = np.kron(turned, eye)
            blocks[1, a, slot, :, half] = np.kron(eye, turned)
    return blocks.reshape(8 * SQUARE, CH)


def expand(blocks, outs):
    for out in outs[:4]:
        out[...] = jnp.zeros_like(out)
    for axis in range(2):
        for a in range(2):
            for slot in range(2):
                part = blocks[pl.ds(((axis * 2 + a) * 2 + slot) * SQUARE, SQUARE), :]
                high = part.astype(jnp.bfloat16)
                low = (part - high.astype(jnp.float32)).astype(jnp.bfloat16)
                if axis == 1 and len(outs) > 4:
                    at = pl.ds(slot * SQUARE, SQUARE), pl.ds(a * CH, CH)
                    outs[4][at] = high
                    outs[5][at] = low
                for k in range(2):
                    rows = pl.ds(slot * CH + k * SQUARE, SQUARE)
                    columns = pl.ds((2 * a + k) * CH, CH)
                    outs[2 * axis][rows, columns] = high
                    outs[2 * axis + 1][rows, columns] = low


VMEM = pl.BlockSpec(memory_space=pltpu.VMEM)
HBM = pl.BlockSpec(memory_space=pltpu.HBM)


def limits(mib=6):
    return pltpu.CompilerParams(vmem_limit_bytes=mib * 1024 * 1024)


def load_kernel(angles, blocks, near_angles, *rest):
    sem = rest[-1]
    copy = pltpu.make_async_copy(angles, near_angles, sem)
    copy.start()
    expand(blocks, rest[:-1])
    copy.wait()


def load(angles):
    part = jax.ShapeDtypeStruct((2 * CH, 4 * CH), jnp.bfloat16)
    return pl.pallas_call(
        load_kernel,
        out_shape=[jax.ShapeDtypeStruct(angles.shape, angles.dtype)] + [part] * 4
        + [jax.ShapeDtypeStruct((CH, 2 * CH), jnp.bfloat16)] * 2,
        in_specs=[HBM, VMEM],
        out_specs=[VMEM] * 7,
        scratch_shapes=[pltpu.SemaphoreType.DMA(())],
        compiler_params=limits(),
        cost_estimate=pl.CostEstimate(
            flops=0, bytes_accessed=4 * 1024 * 1024, transcendentals=0
        ),
    )(angles, jnp.asarray(child_blocks()))


def tables_kernel(blocks, *outs):
    expand(blocks, outs)


def make_tables(blocks):
    part = jax.ShapeDtypeStruct((2 * CH, 4 * CH), jnp.bfloat16)
    return pl.pallas_call(
        tables_kernel,
        out_shape=[part] * 4,
        in_specs=[VMEM],
        out_specs=[VMEM] * 4,
        compiler_params=limits(),
        cost_estimate=pl.CostEstimate(flops=0, bytes_accessed=1024 * 1024, transcendentals=0),
    )(blocks)


def take_kernel(rows, weights, *rest):
    outs, sems = rest[:-1], rest[-1]
    copies = []
    for out, parts in zip(outs, rows()):
        at = 0
        for row, n in parts:
            copies.append(
                pltpu.make_async_copy(
                    weights.at[pl.ds(row, n)], out.at[pl.ds(at, n)], sems.at[len(copies)]
                )
            )
            at += n
    for copy in copies:
        copy.start()
    for copy in copies:
        copy.wait()


def take(weights, rows, sizes, parts):
    return pl.pallas_call(
        functools.partial(take_kernel, rows),
        out_shape=[jax.ShapeDtypeStruct((n, CH), jnp.float32) for n in sizes],
        in_specs=[HBM],
        out_specs=[VMEM] * len(sizes),
        scratch_shapes=[pltpu.SemaphoreType.DMA((parts,))],
        compiler_params=limits(),
        cost_estimate=pl.CostEstimate(
            flops=20_000_000_000, bytes_accessed=4 * 1024 * 1024, transcendentals=0
        ),
    )(weights)


def own_bit(k):
    axis = ("gx", "gy")[k % 2]
    bit = lax.axis_size(axis).bit_length() - 2 - k // 2
    return lax.axis_index(axis) >> bit & 1


def turn(y, angle):
    c, s = cos_sin(angle)
    re, im = y[:, :CH], y[:, CH:]
    u = c * re - s * im
    v = s * re + c * im
    left = lax.broadcasted_iota(jnp.int32, u.shape, 1) < SQUARE
    return jnp.where(left, u, v) + pltpu.roll(jnp.where(left, v, u), SQUARE, 1)


def level_kernel(level, segments, tile, own, arr, ang, high, low, out, scratch):
    upper = own_bit(level) == 1

    def piece(parts):
        count = sum(n for *_, n in parts)
        near, far = (
            jnp.concatenate([ref[pl.ds(row[k], row[4]), :] for row in parts], axis=0)
            for k, ref in ((0, own), (1, arr))
        )
        x = jnp.concatenate([jnp.where(upper, far, near), jnp.where(upper, near, far)], axis=1)
        x_hi = x.astype(jnp.bfloat16)
        x_lo = (x - x_hi.astype(jnp.float32)).astype(jnp.bfloat16)
        dot = functools.partial(jnp.dot, preferred_element_type=jnp.float32)
        y = dot(x_hi, high[...]) + (dot(x_lo, high[...]) + dot(x_hi, low[...]))
        at = 0
        for _, _, row, _, n in parts:
            scratch[pl.ds(2 * at, 2 * n), :] = ang[pl.ds(row, 2 * n), :].astype(jnp.float32)
            at += n
        for a in range(2):
            turned = turn(
                y[:, 2 * a * CH : 2 * (a + 1) * CH], scratch[pl.ds(a, count, stride=2), :]
            )
            at = 0
            for _, _, _, row, n in parts:
                out[pl.ds(row + a, n, stride=2), :] = turned[at : at + n]
                at += n

    parts = segments()
    if len(parts) > 1 or parts[0][4] == tile:
        piece(parts)
        return

    for row_own, row_arr, row_ang, row_out, n in parts:

        def step(i):
            b = pl.multiple_of(i * tile, tile)
            piece([(row_own + b, row_arr + b, row_ang + 2 * b, row_out + 2 * b, tile)])

        pl.loop(0, n // tile)(step)


def level_call(level, segments, own, arr, ang, table, rows, weight=0):
    steps = -(-rows // 512)
    tile = rows // 2 // steps
    kernel = functools.partial(level_kernel, level, segments, tile)
    scratch = [pltpu.VMEM((2 * tile, CH), jnp.float32)]
    return pl.pallas_call(
        kernel,
        out_shape=jax.ShapeDtypeStruct((rows, CH), jnp.float32),
        in_specs=[VMEM] * 5,
        out_specs=VMEM,
        scratch_shapes=scratch,
        compiler_params=limits(),
        cost_estimate=pl.CostEstimate(
            flops=weight * 1_000_000_000, bytes_accessed=rows * 8 * 1024, transcendentals=0
        ),
    )(own, arr, ang, *table)


def fetch_kernel(row, far, near, sem):
    copy = pltpu.make_async_copy(far.at[pl.ds(row, near.shape[0])], near, sem)
    copy.start()
    copy.wait()


def fetch(far, row, rows):
    return pl.pallas_call(
        functools.partial(fetch_kernel, row),
        out_shape=jax.ShapeDtypeStruct((rows, CH), far.dtype),
        in_specs=[pl.BlockSpec(memory_space=pl.ANY)],
        out_specs=VMEM,
        scratch_shapes=[pltpu.SemaphoreType.DMA(())],
        compiler_params=limits(),
        cost_estimate=pl.CostEstimate(flops=0, bytes_accessed=1024 * 1024, transcendentals=0),
    )(far)


def direct_kernel(row, own, arr, ang, high, low, *rest):
    out, scratch, near_out, sems = rest[-4:]
    count, rows = near_out.shape[:2]
    tile = rows // 2
    copies = []
    for i in range(count):
        at = i * tile
        part = near_out.at[i]
        segment = (row + at, at, 2 * (row + at), 0, tile)
        level_kernel(3, lambda: [segment], tile, own, arr, ang, high, low, part, scratch)
        copy = pltpu.make_async_copy(
            part, out.at[pl.ds(2 * (row + at), rows)], sems.at[i]
        )
        copy.start()
        copies.append(copy)
    for copy in copies:
        copy.wait()


def direct_call(own, arr, ang, table, row, boxes):
    rows = arr.shape[0]
    count = -(-rows // 256)
    tile = rows // count
    return pl.pallas_call(
        functools.partial(direct_kernel, row),
        out_shape=jax.ShapeDtypeStruct((boxes, CH), jnp.float32),
        in_specs=[VMEM] * 5,
        out_specs=HBM,
        scratch_shapes=[
            pltpu.VMEM((2 * tile, CH), jnp.float32),
            pltpu.VMEM((count, 2 * tile, CH), jnp.float32),
            pltpu.SemaphoreType.DMA((count,)),
        ],
        compiler_params=limits(),
        cost_estimate=pl.CostEstimate(
            flops=0, bytes_accessed=rows * 8 * 1024, transcendentals=0
        ),
    )(own, arr, ang, *table)


def spread_last(x, high, low, scratch):
    n = x.shape[0]
    x_hi = x.astype(jnp.bfloat16)
    x_lo = (x - x_hi.astype(jnp.float32)).astype(jnp.bfloat16)
    dot = functools.partial(jnp.dot, preferred_element_type=jnp.float32)
    y = dot(x_hi, high[...]) + (dot(x_lo, high[...]) + dot(x_hi, low[...]))
    for a in range(2):
        scratch[pl.ds(a, n, stride=2), :] = y[:, a * CH : (a + 1) * CH]
    return scratch[...]


def before_kernel(row, tile, own, ang, high, low, part, cos_out, sin_out, scratch):
    upper = own_bit(3) == 1

    def step(i):
        rows = pl.ds(pl.multiple_of(2 * i * tile, 2 * tile), 2 * tile)
        near = pl.ds(pl.multiple_of(row + i * tile, tile), tile)
        y = spread_last(own[near, :], high, low, scratch)
        at = pl.ds(pl.multiple_of(2 * (row + i * tile), 2 * tile), 2 * tile)
        c, s = cos_sin(ang[at, :].astype(jnp.float32))
        left = lax.broadcasted_iota(jnp.int32, c.shape, 1) < SQUARE
        c_far, s_far = pltpu.roll(c, SQUARE, 1), pltpu.roll(s, SQUARE, 1)
        c0, c1 = jnp.where(left, c, c_far), jnp.where(left, c_far, c)
        s0, s1 = jnp.where(left, -s, s_far), jnp.where(left, -s_far, s)
        part[rows, :] = jnp.where(upper, c1, c0) * y + jnp.where(upper, s1, s0) * pltpu.roll(
            y, SQUARE, 1
        )
        cos_out[rows, :] = jnp.where(upper, c0, c1)
        sin_out[rows, :] = jnp.where(upper, s0, s1)

    pl.loop(0, part.shape[0] // (2 * tile))(step)


def before_call(own, ang, table, row):
    tile = 128
    part = jax.ShapeDtypeStruct((2 * (own.shape[0] - row), CH), jnp.float32)
    return pl.pallas_call(
        functools.partial(before_kernel, row, tile),
        out_shape=[part] * 3,
        in_specs=[VMEM] * 4,
        out_specs=[VMEM] * 3,
        scratch_shapes=[pltpu.VMEM((2 * tile, CH), jnp.float32)],
        compiler_params=limits(),
        cost_estimate=pl.CostEstimate(
            flops=0, bytes_accessed=4 * 1024 * 1024, transcendentals=0
        ),
    )(own, ang, *table)


def last_kernel(row, arr, part, cos_in, sin_in, high, low, *rest):
    out, scratch, near_out, sems = rest[-4:]
    count, rows = near_out.shape[:2]
    tile = rows // 2
    copies = []
    for i in range(count):
        at = pl.ds(i * rows, rows)
        y = spread_last(arr[pl.ds(i * tile, tile), :], high, low, scratch)
        near_out[i] = (
            part[at, :] + cos_in[at, :] * y + sin_in[at, :] * pltpu.roll(y, SQUARE, 1)
        )
        copy = pltpu.make_async_copy(
            near_out.at[i], out.at[pl.ds(2 * row + i * rows, rows)], sems.at[i]
        )
        copy.start()
        copies.append(copy)
    for copy in copies:
        copy.wait()


def last_call(arr, ready, table, row, earlier):
    rows = arr.shape[0]
    tile = 128
    count = rows // tile
    operands = [arr, *ready, *table, earlier]
    return pl.pallas_call(
        functools.partial(last_kernel, row),
        out_shape=jax.ShapeDtypeStruct(earlier.shape, jnp.float32),
        in_specs=[VMEM] * 6 + [HBM],
        out_specs=HBM,
        scratch_shapes=[
            pltpu.VMEM((2 * tile, CH), jnp.float32),
            pltpu.VMEM((count, 2 * tile, CH), jnp.float32),
            pltpu.SemaphoreType.DMA((count,)),
        ],
        input_output_aliases={6: 0},
        compiler_params=limits(),
        cost_estimate=pl.CostEstimate(
            flops=0, bytes_accessed=rows * 8 * 1024, transcendentals=0
        ),
    )(*operands)


def from_partner(block, axis, bit):
    count = lax.axis_size(axis)
    route = [(low, low ^ (1 << bit)) for low in range(count)]
    return lax.ppermute(block, axis, route)


def after(value, *others):
    return lax.optimization_barrier((value, *others))[0]


def shards(weights, angles):
    bits_x = lax.axis_size("gx").bit_length() - 1
    bits_y = lax.axis_size("gy").bit_length() - 1
    boxes = weights.shape[2]
    base = boxes // 16
    far = weights.reshape(boxes, CH)
    ang, *ready = load(angles.reshape(4 * boxes, CH))
    w2 = far
    tab_x, tab_y, tab_last = ready[:2], ready[2:4], ready[4:]
    env = [ang, tab_x, tab_y, w2]
    ang_far = angles.reshape(4 * boxes, CH)
    aligned = lambda row: pl.multiple_of(row, 16)

    def target(k, other):
        return 1 - own_bit(k) if other else own_bit(k)

    def first(chunks, given):
        def rows():
            low = [target(3, given) + 2 * t for t in range(4)]
            return [
                [(aligned(((1 - own_bit(0)) * 8 + k) * base + at), n) for k in low]
                for at, n in chunks
            ]

        taken = take(far, rows, [4 * n for _, n in chunks], 4 * len(chunks))
        return [from_partner(part, "gx", bits_x - 1) for part in taken]

    def level0(chunk, given, arr, send, weight=0):
        at, n = chunk

        def segments():
            t1, t3 = target(1, send), target(3, given)
            parts = []
            for t2 in range(2):
                low = (t1 * 2 + t2) * 2 + t3
                parts.append(
                    (
                        aligned((own_bit(0) * 8 + low) * base + at),
                        aligned((t1 * 2 + t2) * n),
                        aligned(low * 2 * base + 2 * at),
                        t2 * 2 * n,
                        n,
                    )
                )
            return parts

        return level_call(0, segments, env[3], arr, env[0], env[1], 4 * n, weight)

    def level1(chunk, given, own, arr, send, weight=0):
        at, n = chunk

        def segments():
            t2, t3 = target(2, send), target(3, given)
            row = aligned(t2 * 2 * n)
            return [(row, row, aligned(boxes + (t2 * 2 + t3) * 4 * base + 4 * at), 0, 2 * n)]

        return level_call(1, segments, own, arr, env[0], env[2], 4 * n, weight)

    def level2(chunk, given, own, arr, weight=0):
        at, n = chunk

        def segments():
            t3 = target(3, given)
            return [(0, 0, aligned(2 * boxes + t3 * 8 * base + 8 * at), 0, 4 * n)]

        return level_call(2, segments, own, arr, env[0], env[1], 8 * n, weight)

    def swap1(part):
        return from_partner(part, "gy", bits_y - 1)

    def swap2(part):
        return from_partner(part, "gx", bits_x - 2)

    def swap3(part):
        return from_partner(part, "gy", bits_y - 2)

    cut = base // 2
    a, b, k = (0, cut), (cut, base - cut), (0, base)
    arr_a, arr_b = first([a, b], True)
    send_a = level0(a, True, arr_a, True, AHEAD)
    arr1_a = swap1(send_a)
    keep_a = level0(a, True, after(arr_a, send_a), False, AHEAD)
    send_b = level0(b, True, after(arr_b, keep_a), True)
    arr1_b = swap1(send_b)
    send_a = level1(a, True, keep_a, after(arr1_a, send_b), True, AHEAD)
    arr2_a = swap2(send_a)
    keep_b = level0(b, True, after(arr_b, send_a), False)
    send_b = level1(b, True, keep_b, arr1_b, True)
    arr2_b = swap2(send_b)
    keep_b = level1(b, True, keep_b, arr1_b, False)
    keep_a = level1(a, True, keep_a, arr1_a, False)
    given_a = level2(a, True, keep_a, after(arr2_a, send_b))
    z_a = swap3(given_a)

    given_b = level2(b, True, keep_b, arr2_b)
    z_b = swap3(given_b)

    here = after(lax.axis_index("gx"), given_b[0, 0]) < lax.axis_size("gx")

    def beside(w2, ang, blocks):
        nonlocal far
        far = w2
        ready = make_tables(blocks)
        env[:] = [ang, ready[:2], ready[2:], w2]
        (arr_k,) = first([k], False)
        arr1_k = swap1(level0(k, False, arr_k, True))
        keep_k = level0(k, False, arr_k, False)
        arr2_k = swap2(level1(k, False, keep_k, arr1_k, True))
        keep_k = level1(k, False, keep_k, arr1_k, False)
        return level2(k, False, keep_k, arr2_k)

    kept = lax.cond(
        here, beside, lambda *_: jnp.zeros((8 * base, CH)), far, ang_far, jnp.asarray(child_blocks())
    )
    near_ang = fetch(after(ang_far, kept), 3 * boxes, boxes)
    kept = after(kept, near_ang)
    done = before_call(kept, near_ang, tab_last, 8 * cut)
    out = direct_call(after(kept, done[0]), z_a, near_ang, tab_y, 0, boxes)
    out = last_call(z_b, done, tab_last, 8 * cut, out)
    return out.reshape(1, 1, boxes, CH)


def solution(mesh):
    return jax.shard_map(
        shards,
        mesh=mesh,
        in_specs=(P("gx", "gy", None, None), P(None, "gx", "gy", None, None)),
        out_specs=P("gx", "gy", None, None),
        check_vma=False,
    )
```

```python
import functools

import jax
import jax.numpy as jnp
import ml_dtypes
import numpy as np
from jax import lax
from jax.experimental import pallas as pl
from jax.experimental.pallas import tpu as pltpu
from jax.sharding import PartitionSpec as P

P_SIZE = 8
SQUARE = P_SIZE * P_SIZE
CH = 2 * SQUARE

def half_angle_polys():
    nodes = np.cos((2 * np.arange(64) + 1) * np.pi / 128)
    top = 3.15**2
    u = (nodes + 1) / 2 * top
    x = np.sqrt(u)
    fit = np.polynomial.chebyshev.Chebyshev.fit
    power = np.polynomial.Polynomial
    sine = fit(u, np.sin(x / 2) / x, 5, domain=[0, top]).convert(kind=power)
    cosine = fit(u, 2 * np.cos(x / 2), 6, domain=[0, top]).convert(kind=power)
    return [float(v) for v in sine.coef], [float(v) for v in cosine.coef]


SINE, COSINE = half_angle_polys()


def horner(coef, u):
    total = jnp.full_like(u, coef[-1])
    for c in coef[-2::-1]:
        total = total * u + c
    return total


def cos_sin(x):
    u = x * x
    s = x * horner(SINE, u)
    c2 = horner(COSINE, u)
    return 1.0 - 2.0 * (s * s), s * c2


def child_tables(degree_count):
    cheb_nodes = np.cos((2.0 * np.arange(degree_count) + 1.0) * np.pi / (2.0 * degree_count))
    lagrange = np.ones((2, degree_count, degree_count))
    for parity in range(2):
        points = (cheb_nodes + (2.0 * parity - 1.0)) / 2.0
        for target in range(degree_count):
            for source in range(degree_count):
                for others in range(degree_count):
                    if others != source:
                        lagrange[parity, target, source] *= (
                            points[target] - cheb_nodes[others]
                        ) / (cheb_nodes[source] - cheb_nodes[others])
    return lagrange


def child_blocks():
    lagrange = child_tables(P_SIZE).astype(np.float32)
    eye = np.eye(P_SIZE, dtype=np.float32)
    blocks = np.zeros((2, 2, 2, SQUARE, CH), np.float32)
    for a in range(2):
        turned = lagrange[a].T
        for slot in range(2):
            half = slice(slot * SQUARE, (slot + 1) * SQUARE)
            blocks[0, a, slot, :, half] = np.kron(turned, eye)
            blocks[1, a, slot, :, half] = np.kron(eye, turned)
    return blocks.reshape(8 * SQUARE, CH)


def expand(blocks, outs):
    for out in outs[:4]:
        out[...] = jnp.zeros_like(out)
    for axis in range(2):
        for a in range(2):
            for slot in range(2):
                part = blocks[pl.ds(((axis * 2 + a) * 2 + slot) * SQUARE, SQUARE), :]
                high = part.astype(jnp.bfloat16)
                low = (part - high.astype(jnp.float32)).astype(jnp.bfloat16)
                if axis == 1 and len(outs) > 4:
                    at = pl.ds(slot * SQUARE, SQUARE), pl.ds(a * CH, CH)
                    outs[4][at] = high
                    outs[5][at] = low
                for k in range(2):
                    rows = pl.ds(slot * CH + k * SQUARE, SQUARE)
                    columns = pl.ds((2 * a + k) * CH, CH)
                    outs[2 * axis][rows, columns] = high
                    outs[2 * axis + 1][rows, columns] = low


VMEM = pl.BlockSpec(memory_space=pltpu.VMEM)
HBM = pl.BlockSpec(memory_space=pltpu.HBM)


def limits(mib=6):
    return pltpu.CompilerParams(vmem_limit_bytes=mib * 1024 * 1024)


def load_kernel(angles, blocks, near_angles, *rest):
    sem = rest[-1]
    copy = pltpu.make_async_copy(angles, near_angles, sem)
    copy.start()
    expand(blocks, rest[:-1])
    copy.wait()


def load(angles):
    part = jax.ShapeDtypeStruct((2 * CH, 4 * CH), jnp.bfloat16)
    return pl.pallas_call(
        load_kernel,
        out_shape=[jax.ShapeDtypeStruct(angles.shape, angles.dtype)] + [part] * 4
        + [jax.ShapeDtypeStruct((CH, 2 * CH), jnp.bfloat16)] * 2,
        in_specs=[HBM, VMEM],
        out_specs=[VMEM] * 7,
        scratch_shapes=[pltpu.SemaphoreType.DMA(())],
        compiler_params=limits(),
        cost_estimate=pl.CostEstimate(
            flops=0, bytes_accessed=4 * 1024 * 1024, transcendentals=0
        ),
    )(angles, jnp.asarray(child_blocks()))


def tables_kernel(blocks, *outs):
    expand(blocks, outs)


def make_tables(blocks):
    part = jax.ShapeDtypeStruct((2 * CH, 4 * CH), jnp.bfloat16)
    return pl.pallas_call(
        tables_kernel,
        out_shape=[part] * 4,
        in_specs=[VMEM],
        out_specs=[VMEM] * 4,
        compiler_params=limits(),
        cost_estimate=pl.CostEstimate(flops=0, bytes_accessed=1024 * 1024, transcendentals=0),
    )(blocks)


def take_kernel(pick, chunks, weights, *rest):
    outs, sems = rest[:-1], rest[-1]
    t0, t3 = pick()
    copies = [
        pltpu.make_async_copy(weights.at[t0, :, t3, pl.ds(at, n), :], out, sems.at[i])
        for i, ((at, n), out) in enumerate(zip(chunks, outs))
    ]
    for copy in copies:
        copy.start()
    for copy in copies:
        copy.wait()


def take(weights, pick, chunks):
    return pl.pallas_call(
        functools.partial(take_kernel, pick, chunks),
        out_shape=[
            jax.ShapeDtypeStruct((weights.shape[1], n, CH), jnp.float32) for _, n in chunks
        ],
        in_specs=[HBM],
        out_specs=[VMEM] * len(chunks),
        scratch_shapes=[pltpu.SemaphoreType.DMA((len(chunks),))],
        compiler_params=limits(),
        cost_estimate=pl.CostEstimate(
            flops=20_000_000_000, bytes_accessed=4 * 1024 * 1024, transcendentals=0
        ),
    )(weights)


def own_bit(k):
    axis = ("gx", "gy")[k % 2]
    bit = lax.axis_size(axis).bit_length() - 2 - k // 2
    return lax.axis_index(axis) >> bit & 1


def turn(y, angle):
    c, s = cos_sin(angle)
    re, im = y[:, :CH], y[:, CH:]
    u = c * re - s * im
    v = s * re + c * im
    left = lax.broadcasted_iota(jnp.int32, u.shape, 1) < SQUARE
    return jnp.where(left, u, v) + pltpu.roll(jnp.where(left, v, u), SQUARE, 1)


def level_kernel(level, segments, tile, own, arr, ang, high, low, out, scratch):
    upper = own_bit(level) == 1

    def piece(parts):
        count = sum(n for *_, n in parts)
        near, far = (
            jnp.concatenate([ref[pl.ds(row[k], row[4]), :] for row in parts], axis=0)
            for k, ref in ((0, own), (1, arr))
        )
        x = jnp.concatenate([jnp.where(upper, far, near), jnp.where(upper, near, far)], axis=1)
        x_hi = x.astype(jnp.bfloat16)
        x_lo = (x - x_hi.astype(jnp.float32)).astype(jnp.bfloat16)
        dot = functools.partial(jnp.dot, preferred_element_type=jnp.float32)
        y = dot(x_hi, high[...]) + (dot(x_lo, high[...]) + dot(x_hi, low[...]))
        at = 0
        for _, _, row, _, n in parts:
            scratch[pl.ds(2 * at, 2 * n), :] = ang[pl.ds(row, 2 * n), :].astype(jnp.float32)
            at += n
        for a in range(2):
            turned = turn(
                y[:, 2 * a * CH : 2 * (a + 1) * CH], scratch[pl.ds(a, count, stride=2), :]
            )
            at = 0
            for _, _, _, row, n in parts:
                out[pl.ds(row + a, n, stride=2), :] = turned[at : at + n]
                at += n

    parts = segments()
    if len(parts) > 1 or parts[0][4] == tile:
        piece(parts)
        return

    for row_own, row_arr, row_ang, row_out, n in parts:

        def step(i):
            b = pl.multiple_of(i * tile, tile)
            piece([(row_own + b, row_arr + b, row_ang + 2 * b, row_out + 2 * b, tile)])

        pl.loop(0, n // tile)(step)


def level_call(level, segments, own, arr, ang, table, rows):
    steps = -(-rows // 512)
    tile = rows // 2 // steps
    kernel = functools.partial(level_kernel, level, segments, tile)
    scratch = [pltpu.VMEM((2 * tile, CH), jnp.float32)]
    return pl.pallas_call(
        kernel,
        out_shape=jax.ShapeDtypeStruct((rows, CH), jnp.float32),
        in_specs=[VMEM] * 5,
        out_specs=VMEM,
        scratch_shapes=scratch,
        compiler_params=limits(),
        cost_estimate=pl.CostEstimate(
            flops=0, bytes_accessed=rows * 8 * 1024, transcendentals=0
        ),
    )(own, arr, ang, *table)


def fetch_kernel(row, far, near, sem):
    copy = pltpu.make_async_copy(far.at[pl.ds(row, near.shape[0])], near, sem)
    copy.start()
    copy.wait()


def fetch(far, row, rows):
    return pl.pallas_call(
        functools.partial(fetch_kernel, row),
        out_shape=jax.ShapeDtypeStruct((rows, CH), far.dtype),
        in_specs=[pl.BlockSpec(memory_space=pl.ANY)],
        out_specs=VMEM,
        scratch_shapes=[pltpu.SemaphoreType.DMA(())],
        compiler_params=limits(),
        cost_estimate=pl.CostEstimate(flops=0, bytes_accessed=1024 * 1024, transcendentals=0),
    )(far)


def direct_kernel(row, own, arr, ang, high, low, *rest):
    out, scratch, near_out, sems = rest[-4:]
    count, rows = near_out.shape[:2]
    tile = rows // 2
    copies = []
    for i in range(count):
        at = i * tile
        part = near_out.at[i]
        segment = (row + at, at, 2 * (row + at), 0, tile)
        level_kernel(3, lambda: [segment], tile, own, arr, ang, high, low, part, scratch)
        copy = pltpu.make_async_copy(
            part, out.at[pl.ds(2 * (row + at), rows)], sems.at[i]
        )
        copy.start()
        copies.append(copy)
    for copy in copies:
        copy.wait()


def direct_call(own, arr, ang, table, row, boxes):
    rows = arr.shape[0]
    count = -(-rows // 256)
    tile = rows // count
    return pl.pallas_call(
        functools.partial(direct_kernel, row),
        out_shape=jax.ShapeDtypeStruct((boxes, CH), jnp.float32),
        in_specs=[VMEM] * 5,
        out_specs=HBM,
        scratch_shapes=[
            pltpu.VMEM((2 * tile, CH), jnp.float32),
            pltpu.VMEM((count, 2 * tile, CH), jnp.float32),
            pltpu.SemaphoreType.DMA((count,)),
        ],
        compiler_params=limits(),
        cost_estimate=pl.CostEstimate(
            flops=0, bytes_accessed=rows * 8 * 1024, transcendentals=0
        ),
    )(own, arr, ang, *table)


def spread_last(x, high, low, scratch):
    n = x.shape[0]
    x_hi = x.astype(jnp.bfloat16)
    x_lo = (x - x_hi.astype(jnp.float32)).astype(jnp.bfloat16)
    dot = functools.partial(jnp.dot, preferred_element_type=jnp.float32)
    y = dot(x_hi, high[...]) + (dot(x_lo, high[...]) + dot(x_hi, low[...]))
    for a in range(2):
        scratch[pl.ds(a, n, stride=2), :] = y[:, a * CH : (a + 1) * CH]
    return scratch[...]


def before_kernel(row, tile, own, ang, high, low, part, cos_out, sin_out, scratch):
    upper = own_bit(3) == 1

    def step(i):
        rows = pl.ds(pl.multiple_of(2 * i * tile, 2 * tile), 2 * tile)
        near = pl.ds(pl.multiple_of(row + i * tile, tile), tile)
        y = spread_last(own[near, :], high, low, scratch)
        at = pl.ds(pl.multiple_of(2 * (row + i * tile), 2 * tile), 2 * tile)
        c, s = cos_sin(ang[at, :].astype(jnp.float32))
        left = lax.broadcasted_iota(jnp.int32, c.shape, 1) < SQUARE
        c_far, s_far = pltpu.roll(c, SQUARE, 1), pltpu.roll(s, SQUARE, 1)
        c0, c1 = jnp.where(left, c, c_far), jnp.where(left, c_far, c)
        s0, s1 = jnp.where(left, -s, s_far), jnp.where(left, -s_far, s)
        part[rows, :] = jnp.where(upper, c1, c0) * y + jnp.where(upper, s1, s0) * pltpu.roll(
            y, SQUARE, 1
        )
        cos_out[rows, :] = jnp.where(upper, c0, c1)
        sin_out[rows, :] = jnp.where(upper, s0, s1)

    pl.loop(0, part.shape[0] // (2 * tile))(step)


def before_call(own, ang, table, row):
    tile = 128
    part = jax.ShapeDtypeStruct((2 * (own.shape[0] - row), CH), jnp.float32)
    return pl.pallas_call(
        functools.partial(before_kernel, row, tile),
        out_shape=[part] * 3,
        in_specs=[VMEM] * 4,
        out_specs=[VMEM] * 3,
        scratch_shapes=[pltpu.VMEM((2 * tile, CH), jnp.float32)],
        compiler_params=limits(),
        cost_estimate=pl.CostEstimate(
            flops=0, bytes_accessed=4 * 1024 * 1024, transcendentals=0
        ),
    )(own, ang, *table)


def last_kernel(row, arr, part, cos_in, sin_in, high, low, *rest):
    out, scratch, near_out, sems = rest[-4:]
    count, rows = near_out.shape[:2]
    tile = rows // 2
    copies = []
    for i in range(count):
        at = pl.ds(i * rows, rows)
        y = spread_last(arr[pl.ds(i * tile, tile), :], high, low, scratch)
        near_out[i] = (
            part[at, :] + cos_in[at, :] * y + sin_in[at, :] * pltpu.roll(y, SQUARE, 1)
        )
        copy = pltpu.make_async_copy(
            near_out.at[i], out.at[pl.ds(2 * row + i * rows, rows)], sems.at[i]
        )
        copy.start()
        copies.append(copy)
    for copy in copies:
        copy.wait()


def last_call(arr, ready, table, row, earlier):
    rows = arr.shape[0]
    tile = 128
    count = rows // tile
    operands = [arr, *ready, *table, earlier]
    return pl.pallas_call(
        functools.partial(last_kernel, row),
        out_shape=jax.ShapeDtypeStruct(earlier.shape, jnp.float32),
        in_specs=[VMEM] * 6 + [HBM],
        out_specs=HBM,
        scratch_shapes=[
            pltpu.VMEM((2 * tile, CH), jnp.float32),
            pltpu.VMEM((count, 2 * tile, CH), jnp.float32),
            pltpu.SemaphoreType.DMA((count,)),
        ],
        input_output_aliases={6: 0},
        compiler_params=limits(),
        cost_estimate=pl.CostEstimate(
            flops=0, bytes_accessed=rows * 8 * 1024, transcendentals=0
        ),
    )(*operands)


def from_partner(block, axis, bit):
    count = lax.axis_size(axis)
    route = [(low, low ^ (1 << bit)) for low in range(count)]
    return lax.ppermute(block, axis, route)


def after(value, *others):
    return lax.optimization_barrier((value, *others))[0]


def shards(weights, angles):
    bits_x = lax.axis_size("gx").bit_length() - 1
    bits_y = lax.axis_size("gy").bit_length() - 1
    boxes = weights.shape[2]
    base = boxes // 16
    far = weights.reshape(boxes, CH)
    ang, *ready = load(angles.reshape(4 * boxes, CH))
    w2 = far
    tab_x, tab_y, tab_last = ready[:2], ready[2:4], ready[4:]
    env = [ang, tab_x, tab_y, w2]
    ang_far = angles.reshape(4 * boxes, CH)
    aligned = lambda row: pl.multiple_of(row, 16)

    def target(k, other):
        return 1 - own_bit(k) if other else own_bit(k)

    def first(chunks, given):
        def pick():
            return 1 - own_bit(0), target(3, given)

        taken = take(far.reshape(2, 4, 2, base, CH), pick, chunks)
        return [from_partner(part.reshape(-1, CH), "gx", bits_x - 1) for part in taken]

    def level0(chunk, given, arr, send):
        at, n = chunk

        def segments():
            t1, t3 = target(1, send), target(3, given)
            parts = []
            for t2 in range(2):
                low = (t1 * 2 + t2) * 2 + t3
                parts.append(
                    (
                        aligned((own_bit(0) * 8 + low) * base + at),
                        aligned((t1 * 2 + t2) * n),
                        aligned(low * 2 * base + 2 * at),
                        t2 * 2 * n,
                        n,
                    )
                )
            return parts

        return level_call(0, segments, env[3], arr, env[0], env[1], 4 * n)

    def level1(chunk, given, own, arr, send):
        at, n = chunk

        def segments():
            t2, t3 = target(2, send), target(3, given)
            row = aligned(t2 * 2 * n)
            return [(row, row, aligned(boxes + (t2 * 2 + t3) * 4 * base + 4 * at), 0, 2 * n)]

        return level_call(1, segments, own, arr, env[0], env[2], 4 * n)

    def level2(chunk, given, own, arr):
        at, n = chunk

        def segments():
            t3 = target(3, given)
            return [(0, 0, aligned(2 * boxes + t3 * 8 * base + 8 * at), 0, 4 * n)]

        return level_call(2, segments, own, arr, env[0], env[1], 8 * n)

    def swap1(part):
        return from_partner(part, "gy", bits_y - 1)

    def swap2(part):
        return from_partner(part, "gx", bits_x - 2)

    def swap3(part):
        return from_partner(part, "gy", bits_y - 2)

    cut = base // 2
    a, b, k = (0, cut), (cut, base - cut), (0, base)
    arr_a, arr_b = first([a, b], True)
    send_a = level0(a, True, arr_a, True)
    arr1_a = swap1(send_a)
    keep_a = level0(a, True, after(arr_a, send_a), False)
    send_b = level0(b, True, after(arr_b, keep_a), True)
    arr1_b = swap1(send_b)
    send_a = level1(a, True, keep_a, after(arr1_a, send_b), True)
    arr2_a = swap2(send_a)
    keep_b = level0(b, True, after(arr_b, send_a), False)
    send_b = level1(b, True, keep_b, arr1_b, True)
    arr2_b = swap2(send_b)
    keep_a = level1(a, True, keep_a, arr1_a, False)
    given_a = level2(a, True, keep_a, after(arr2_a, send_b))
    z_a = swap3(given_a)

    keep_b = level1(b, True, keep_b, after(arr1_b, given_a), False)
    given_b = level2(b, True, keep_b, arr2_b)
    z_b = swap3(given_b)

    here = after(lax.axis_index("gx"), given_b[0, 0]) < lax.axis_size("gx")

    def beside(w2, ang, blocks):
        nonlocal far
        far = w2
        ready = make_tables(blocks)
        env[:] = [ang, ready[:2], ready[2:], w2]
        (arr_k,) = first([k], False)
        arr1_k = swap1(level0(k, False, arr_k, True))
        keep_k = level0(k, False, arr_k, False)
        arr2_k = swap2(level1(k, False, keep_k, arr1_k, True))
        keep_k = level1(k, False, keep_k, arr1_k, False)
        return level2(k, False, keep_k, arr2_k)

    kept = lax.cond(
        here, beside, lambda *_: jnp.zeros((8 * base, CH)), far, ang_far, jnp.asarray(child_blocks())
    )
    near_ang = fetch(after(ang_far, kept), 3 * boxes, boxes)
    kept = after(kept, near_ang)
    done = before_call(kept, near_ang, tab_last, 8 * cut)
    out = direct_call(after(kept, done[0]), z_a, near_ang, tab_y, 0, boxes)
    out = last_call(z_b, done, tab_last, 8 * cut, out)
    return out.reshape(1, 1, boxes, CH)


def solution(mesh):
    return jax.shard_map(
        shards,
        mesh=mesh,
        in_specs=(P("gx", "gy", None, None), P(None, "gx", "gy", None, None)),
        out_specs=P("gx", "gy", None, None),
        check_vma=False,
    )
```

```python
import functools

import jax
import jax.numpy as jnp
import ml_dtypes
import numpy as np
from jax import lax
from jax.experimental import pallas as pl
from jax.experimental.pallas import tpu as pltpu
from jax.sharding import PartitionSpec as P

P_SIZE = 8
SQUARE = P_SIZE * P_SIZE
CH = 2 * SQUARE

def half_angle_polys():
    nodes = np.cos((2 * np.arange(64) + 1) * np.pi / 128)
    top = 3.15**2
    u = (nodes + 1) / 2 * top
    x = np.sqrt(u)
    fit = np.polynomial.chebyshev.Chebyshev.fit
    power = np.polynomial.Polynomial
    sine = fit(u, np.sin(x / 2) / x, 5, domain=[0, top]).convert(kind=power)
    cosine = fit(u, 2 * np.cos(x / 2), 6, domain=[0, top]).convert(kind=power)
    return [float(v) for v in sine.coef], [float(v) for v in cosine.coef]


AHEAD, LAST = 5_000_000_000, 1_500_000_000
SINE, COSINE = half_angle_polys()


def horner(coef, u):
    total = jnp.full_like(u, coef[-1])
    for c in coef[-2::-1]:
        total = total * u + c
    return total


def cos_sin(x):
    u = x * x
    s = x * horner(SINE, u)
    c2 = horner(COSINE, u)
    return 1.0 - 2.0 * (s * s), s * c2


def child_tables(degree_count):
    cheb_nodes = np.cos((2.0 * np.arange(degree_count) + 1.0) * np.pi / (2.0 * degree_count))
    lagrange = np.ones((2, degree_count, degree_count))
    for parity in range(2):
        points = (cheb_nodes + (2.0 * parity - 1.0)) / 2.0
        for target in range(degree_count):
            for source in range(degree_count):
                for others in range(degree_count):
                    if others != source:
                        lagrange[parity, target, source] *= (
                            points[target] - cheb_nodes[others]
                        ) / (cheb_nodes[source] - cheb_nodes[others])
    return lagrange


def child_blocks():
    lagrange = child_tables(P_SIZE).astype(np.float32)
    eye = np.eye(P_SIZE, dtype=np.float32)
    blocks = np.zeros((2, 2, 2, SQUARE, CH), np.float32)
    for a in range(2):
        turned = lagrange[a].T
        for slot in range(2):
            half = slice(slot * SQUARE, (slot + 1) * SQUARE)
            blocks[0, a, slot, :, half] = np.kron(turned, eye)
            blocks[1, a, slot, :, half] = np.kron(eye, turned)
    return blocks.reshape(8 * SQUARE, CH)


def expand(blocks, outs):
    for out in outs[:4]:
        out[...] = jnp.zeros_like(out)
    for axis in range(2):
        for a in range(2):
            for slot in range(2):
                part = blocks[pl.ds(((axis * 2 + a) * 2 + slot) * SQUARE, SQUARE), :]
                high = part.astype(jnp.bfloat16)
                low = (part - high.astype(jnp.float32)).astype(jnp.bfloat16)
                if axis == 1 and len(outs) > 4:
                    at = pl.ds(slot * SQUARE, SQUARE), pl.ds(a * CH, CH)
                    outs[4][at] = high
                    outs[5][at] = low
                for k in range(2):
                    rows = pl.ds(slot * CH + k * SQUARE, SQUARE)
                    columns = pl.ds((2 * a + k) * CH, CH)
                    outs[2 * axis][rows, columns] = high
                    outs[2 * axis + 1][rows, columns] = low


VMEM = pl.BlockSpec(memory_space=pltpu.VMEM)
HBM = pl.BlockSpec(memory_space=pltpu.HBM)


def limits(mib=6):
    return pltpu.CompilerParams(vmem_limit_bytes=mib * 1024 * 1024)


def load_kernel(angles, blocks, near_angles, *rest):
    sem = rest[-1]
    copy = pltpu.make_async_copy(angles, near_angles, sem)
    copy.start()
    expand(blocks, rest[:-1])
    copy.wait()


def load(angles):
    part = jax.ShapeDtypeStruct((2 * CH, 4 * CH), jnp.bfloat16)
    return pl.pallas_call(
        load_kernel,
        out_shape=[jax.ShapeDtypeStruct(angles.shape, angles.dtype)] + [part] * 4
        + [jax.ShapeDtypeStruct((CH, 2 * CH), jnp.bfloat16)] * 2,
        in_specs=[HBM, VMEM],
        out_specs=[VMEM] * 7,
        scratch_shapes=[pltpu.SemaphoreType.DMA(())],
        compiler_params=limits(),
        cost_estimate=pl.CostEstimate(
            flops=0, bytes_accessed=4 * 1024 * 1024, transcendentals=0
        ),
    )(angles, jnp.asarray(child_blocks()))


def tables_kernel(blocks, *outs):
    expand(blocks, outs)


def make_tables(blocks):
    part = jax.ShapeDtypeStruct((2 * CH, 4 * CH), jnp.bfloat16)
    return pl.pallas_call(
        tables_kernel,
        out_shape=[part] * 4,
        in_specs=[VMEM],
        out_specs=[VMEM] * 4,
        compiler_params=limits(),
        cost_estimate=pl.CostEstimate(flops=0, bytes_accessed=1024 * 1024, transcendentals=0),
    )(blocks)


def take_kernel(pick, chunks, weights, *rest):
    outs, sems = rest[:-1], rest[-1]
    t0, t3 = pick()
    copies = [
        pltpu.make_async_copy(weights.at[t0, :, t3, pl.ds(at, n), :], out, sems.at[i])
        for i, ((at, n), out) in enumerate(zip(chunks, outs))
    ]
    for copy in copies:
        copy.start()
    for copy in copies:
        copy.wait()


def take(weights, pick, chunks):
    return pl.pallas_call(
        functools.partial(take_kernel, pick, chunks),
        out_shape=[
            jax.ShapeDtypeStruct((weights.shape[1], n, CH), jnp.float32) for _, n in chunks
        ],
        in_specs=[HBM],
        out_specs=[VMEM] * len(chunks),
        scratch_shapes=[pltpu.SemaphoreType.DMA((len(chunks),))],
        compiler_params=limits(),
        cost_estimate=pl.CostEstimate(
            flops=20_000_000_000, bytes_accessed=4 * 1024 * 1024, transcendentals=0
        ),
    )(weights)


def own_bit(k):
    axis = ("gx", "gy")[k % 2]
    bit = lax.axis_size(axis).bit_length() - 2 - k // 2
    return lax.axis_index(axis) >> bit & 1


def turn(y, angle):
    c, s = cos_sin(angle)
    re, im = y[:, :CH], y[:, CH:]
    u = c * re - s * im
    v = s * re + c * im
    left = lax.broadcasted_iota(jnp.int32, u.shape, 1) < SQUARE
    return jnp.where(left, u, v) + pltpu.roll(jnp.where(left, v, u), SQUARE, 1)


def level_kernel(level, segments, tile, own, arr, ang, high, low, out, scratch):
    upper = own_bit(level) == 1

    def piece(parts):
        count = sum(n for *_, n in parts)
        near, far = (
            jnp.concatenate([ref[pl.ds(row[k], row[4]), :] for row in parts], axis=0)
            for k, ref in ((0, own), (1, arr))
        )
        x = jnp.concatenate([jnp.where(upper, far, near), jnp.where(upper, near, far)], axis=1)
        x_hi = x.astype(jnp.bfloat16)
        x_lo = (x - x_hi.astype(jnp.float32)).astype(jnp.bfloat16)
        dot = functools.partial(jnp.dot, preferred_element_type=jnp.float32)
        y = dot(x_hi, high[...]) + (dot(x_lo, high[...]) + dot(x_hi, low[...]))
        at = 0
        for _, _, row, _, n in parts:
            scratch[pl.ds(2 * at, 2 * n), :] = ang[pl.ds(row, 2 * n), :].astype(jnp.float32)
            at += n
        for a in range(2):
            turned = turn(
                y[:, 2 * a * CH : 2 * (a + 1) * CH], scratch[pl.ds(a, count, stride=2), :]
            )
            at = 0
            for _, _, _, row, n in parts:
                out[pl.ds(row + a, n, stride=2), :] = turned[at : at + n]
                at += n

    parts = segments()
    if len(parts) > 1 or parts[0][4] == tile:
        piece(parts)
        return

    for row_own, row_arr, row_ang, row_out, n in parts:

        def step(i):
            b = pl.multiple_of(i * tile, tile)
            piece([(row_own + b, row_arr + b, row_ang + 2 * b, row_out + 2 * b, tile)])

        pl.loop(0, n // tile)(step)


def level_call(level, segments, own, arr, ang, table, rows, weight=0):
    steps = -(-rows // 512)
    tile = rows // 2 // steps
    kernel = functools.partial(level_kernel, level, segments, tile)
    scratch = [pltpu.VMEM((2 * tile, CH), jnp.float32)]
    return pl.pallas_call(
        kernel,
        out_shape=jax.ShapeDtypeStruct((rows, CH), jnp.float32),
        in_specs=[VMEM] * 5,
        out_specs=VMEM,
        scratch_shapes=scratch,
        compiler_params=limits(),
        cost_estimate=pl.CostEstimate(
            flops=weight, bytes_accessed=rows * 8 * 1024, transcendentals=0
        ),
    )(own, arr, ang, *table)


def fetch_kernel(row, far, near, sem):
    copy = pltpu.make_async_copy(far.at[pl.ds(row, near.shape[0])], near, sem)
    copy.start()
    copy.wait()


def fetch(far, row, rows):
    return pl.pallas_call(
        functools.partial(fetch_kernel, row),
        out_shape=jax.ShapeDtypeStruct((rows, CH), far.dtype),
        in_specs=[pl.BlockSpec(memory_space=pl.ANY)],
        out_specs=VMEM,
        scratch_shapes=[pltpu.SemaphoreType.DMA(())],
        compiler_params=limits(),
        cost_estimate=pl.CostEstimate(flops=0, bytes_accessed=1024 * 1024, transcendentals=0),
    )(far)


def direct_kernel(row, own, arr, ang, high, low, *rest):
    out, scratch, near_out, sems = rest[-4:]
    count, rows = near_out.shape[:2]
    tile = rows // 2
    copies = []
    for i in range(count):
        at = i * tile
        part = near_out.at[i]
        segment = (row + at, at, 2 * (row + at), 0, tile)
        level_kernel(3, lambda: [segment], tile, own, arr, ang, high, low, part, scratch)
        copy = pltpu.make_async_copy(
            part, out.at[pl.ds(2 * (row + at), rows)], sems.at[i]
        )
        copy.start()
        copies.append(copy)
    for copy in copies:
        copy.wait()


def direct_call(own, arr, ang, table, row, boxes):
    rows = arr.shape[0]
    count = -(-rows // 256)
    tile = rows // count
    return pl.pallas_call(
        functools.partial(direct_kernel, row),
        out_shape=jax.ShapeDtypeStruct((boxes, CH), jnp.float32),
        in_specs=[VMEM] * 5,
        out_specs=HBM,
        scratch_shapes=[
            pltpu.VMEM((2 * tile, CH), jnp.float32),
            pltpu.VMEM((count, 2 * tile, CH), jnp.float32),
            pltpu.SemaphoreType.DMA((count,)),
        ],
        compiler_params=limits(),
        cost_estimate=pl.CostEstimate(
            flops=LAST, bytes_accessed=rows * 8 * 1024, transcendentals=0
        ),
    )(own, arr, ang, *table)


def tile_of(rows):
    return next(n for n in (128, 144, 112, 96) if rows % n == 0)


def spread_last(x, high, low, scratch):
    n = x.shape[0]
    x_hi = x.astype(jnp.bfloat16)
    x_lo = (x - x_hi.astype(jnp.float32)).astype(jnp.bfloat16)
    dot = functools.partial(jnp.dot, preferred_element_type=jnp.float32)
    y = dot(x_hi, high[...]) + (dot(x_lo, high[...]) + dot(x_hi, low[...]))
    for a in range(2):
        scratch[pl.ds(a, n, stride=2), :] = y[:, a * CH : (a + 1) * CH]
    return scratch[...]


def before_kernel(row, tile, own, ang, high, low, part, cos_out, sin_out, scratch):
    upper = own_bit(3) == 1

    def step(i):
        rows = pl.ds(pl.multiple_of(2 * i * tile, 2 * tile), 2 * tile)
        near = pl.ds(pl.multiple_of(row + i * tile, 16), tile)
        y = spread_last(own[near, :], high, low, scratch)
        at = pl.ds(pl.multiple_of(2 * (row + i * tile), 32), 2 * tile)
        c, s = cos_sin(ang[at, :].astype(jnp.float32))
        left = lax.broadcasted_iota(jnp.int32, c.shape, 1) < SQUARE
        c_far, s_far = pltpu.roll(c, SQUARE, 1), pltpu.roll(s, SQUARE, 1)
        c0, c1 = jnp.where(left, c, c_far), jnp.where(left, c_far, c)
        s0, s1 = jnp.where(left, -s, s_far), jnp.where(left, -s_far, s)
        part[rows, :] = jnp.where(upper, c1, c0) * y + jnp.where(upper, s1, s0) * pltpu.roll(
            y, SQUARE, 1
        )
        cos_out[rows, :] = jnp.where(upper, c0, c1)
        sin_out[rows, :] = jnp.where(upper, s0, s1)

    pl.loop(0, part.shape[0] // (2 * tile))(step)


def before_call(own, ang, table, row):
    tile = tile_of(own.shape[0] - row)
    part = jax.ShapeDtypeStruct((2 * (own.shape[0] - row), CH), jnp.float32)
    return pl.pallas_call(
        functools.partial(before_kernel, row, tile),
        out_shape=[part] * 3,
        in_specs=[VMEM] * 4,
        out_specs=[VMEM] * 3,
        scratch_shapes=[pltpu.VMEM((2 * tile, CH), jnp.float32)],
        compiler_params=limits(),
        cost_estimate=pl.CostEstimate(
            flops=0, bytes_accessed=4 * 1024 * 1024, transcendentals=0
        ),
    )(own, ang, *table)


def last_kernel(row, arr, part, cos_in, sin_in, high, low, *rest):
    out, scratch, near_out, sems = rest[-4:]
    count, rows = near_out.shape[:2]
    tile = rows // 2
    copies = []
    for i in range(count):
        at = pl.ds(i * rows, rows)
        y = spread_last(arr[pl.ds(i * tile, tile), :], high, low, scratch)
        near_out[i] = (
            part[at, :] + cos_in[at, :] * y + sin_in[at, :] * pltpu.roll(y, SQUARE, 1)
        )
        copy = pltpu.make_async_copy(
            near_out.at[i], out.at[pl.ds(2 * row + i * rows, rows)], sems.at[i]
        )
        copy.start()
        copies.append(copy)
    for copy in copies:
        copy.wait()


def last_call(arr, ready, table, row, earlier):
    rows = arr.shape[0]
    tile = tile_of(rows)
    count = rows // tile
    operands = [arr, *ready, *table, earlier]
    return pl.pallas_call(
        functools.partial(last_kernel, row),
        out_shape=jax.ShapeDtypeStruct(earlier.shape, jnp.float32),
        in_specs=[VMEM] * 6 + [HBM],
        out_specs=HBM,
        scratch_shapes=[
            pltpu.VMEM((2 * tile, CH), jnp.float32),
            pltpu.VMEM((count, 2 * tile, CH), jnp.float32),
            pltpu.SemaphoreType.DMA((count,)),
        ],
        input_output_aliases={6: 0},
        compiler_params=limits(),
        cost_estimate=pl.CostEstimate(
            flops=0, bytes_accessed=rows * 8 * 1024, transcendentals=0
        ),
    )(*operands)


def from_partner(block, axis, bit):
    count = lax.axis_size(axis)
    route = [(low, low ^ (1 << bit)) for low in range(count)]
    return lax.ppermute(block, axis, route)


def after(value, *others):
    return lax.optimization_barrier((value, *others))[0]


def shards(weights, angles):
    bits_x = lax.axis_size("gx").bit_length() - 1
    bits_y = lax.axis_size("gy").bit_length() - 1
    boxes = weights.shape[2]
    base = boxes // 16
    far = weights.reshape(boxes, CH)
    w2 = far
    env = [None] * 4
    ang_far = angles.reshape(4 * boxes, CH)
    aligned = lambda row, by=16: pl.multiple_of(row, by)

    def target(k, other):
        return 1 - own_bit(k) if other else own_bit(k)

    def first(chunks, given):
        def pick():
            return 1 - own_bit(0), target(3, given)

        return [
            part.reshape(-1, CH) for part in take(far.reshape(2, 4, 2, base, CH), pick, chunks)
        ]

    def swap0(part):
        return from_partner(part, "gx", bits_x - 1)

    def level0(chunk, given, arr, send, weight=0):
        at, n = chunk

        def segments():
            t1, t3 = target(1, send), target(3, given)
            parts = []
            for t2 in range(2):
                low = (t1 * 2 + t2) * 2 + t3
                parts.append(
                    (
                        aligned((own_bit(0) * 8 + low) * base + at, 8),
                        aligned((t1 * 2 + t2) * n, 8),
                        aligned(low * 2 * base + 2 * at),
                        t2 * 2 * n,
                        n,
                    )
                )
            return parts

        return level_call(0, segments, env[3], arr, env[0], env[1], 4 * n, weight)

    def level1(chunk, given, own, arr, send, weight=0):
        at, n = chunk

        def segments():
            t2, t3 = target(2, send), target(3, given)
            row = aligned(t2 * 2 * n)
            return [(row, row, aligned(boxes + (t2 * 2 + t3) * 4 * base + 4 * at), 0, 2 * n)]

        return level_call(1, segments, own, arr, env[0], env[2], 4 * n, weight)

    def level2(chunk, given, own, arr):
        at, n = chunk

        def segments():
            t3 = target(3, given)
            return [(0, 0, aligned(2 * boxes + t3 * 8 * base + 8 * at), 0, 4 * n)]

        return level_call(2, segments, own, arr, env[0], env[1], 8 * n)

    def swap1(part):
        return from_partner(part, "gy", bits_y - 1)

    def swap2(part):
        return from_partner(part, "gx", bits_x - 2)

    def swap3(part):
        return from_partner(part, "gy", bits_y - 2)

    cut = 7 * base // 16
    a, b, k = (0, cut), (cut, base - cut), (0, base)
    send_a, send_b = first([a, b], True)
    arr_a, arr_b = swap0(send_a), swap0(send_b)
    ang, *ready = load(after(ang_far, send_a))
    tab_x, tab_y, tab_last = ready[:2], ready[2:4], ready[4:]
    env[:] = [ang, tab_x, tab_y, after(w2, send_b)]
    send_a = level0(a, True, arr_a, True, AHEAD)
    arr1_a = swap1(send_a)
    keep_a = level0(a, True, after(arr_a, send_a), False, AHEAD)
    send_b = level0(b, True, after(arr_b, keep_a), True)
    arr1_b = swap1(send_b)
    send_a = level1(a, True, keep_a, after(arr1_a, send_b), True, AHEAD)
    arr2_a = swap2(send_a)
    keep_b = level0(b, True, after(arr_b, send_a), False)
    send_b = level1(b, True, keep_b, arr1_b, True)
    arr2_b = swap2(send_b)
    keep_a = level1(a, True, keep_a, arr1_a, False)
    given_a = level2(a, True, keep_a, after(arr2_a, send_b))
    z_a = swap3(given_a)

    keep_b = level1(b, True, keep_b, after(arr1_b, given_a), False)
    given_b = level2(b, True, keep_b, arr2_b)
    z_b = swap3(given_b)

    here = after(lax.axis_index("gx"), given_b[0, 0]) < lax.axis_size("gx")

    def beside(w2, ang, blocks):
        nonlocal far
        far = w2
        ready = make_tables(blocks)
        env[:] = [ang, ready[:2], ready[2:], w2]
        arr_k = swap0(first([k], False)[0])
        arr1_k = swap1(level0(k, False, arr_k, True))
        keep_k = level0(k, False, arr_k, False)
        arr2_k = swap2(level1(k, False, keep_k, arr1_k, True))
        keep_k = level1(k, False, keep_k, arr1_k, False)
        return level2(k, False, keep_k, arr2_k)

    kept = lax.cond(
        here, beside, lambda *_: jnp.zeros((8 * base, CH)), far, ang_far, jnp.asarray(child_blocks())
    )
    near_ang = fetch(after(ang_far, kept), 3 * boxes, boxes)
    kept = after(kept, near_ang)
    done = before_call(kept, near_ang, tab_last, 8 * cut)
    out = direct_call(after(kept, done[0]), z_a, near_ang, tab_y, 0, boxes)
    out = last_call(z_b, done, tab_last, 8 * cut, out)
    return out.reshape(1, 1, boxes, CH)


def solution(mesh):
    return jax.shard_map(
        shards,
        mesh=mesh,
        in_specs=(P("gx", "gy", None, None), P(None, "gx", "gy", None, None)),
        out_specs=P("gx", "gy", None, None),
        check_vma=False,
    )
```

```python
import functools

import jax
import jax.numpy as jnp
import ml_dtypes
import numpy as np
from jax import lax
from jax.experimental import pallas as pl
from jax.experimental.pallas import tpu as pltpu
from jax.sharding import PartitionSpec as P

P_SIZE = 8
SQUARE = P_SIZE * P_SIZE
CH = 2 * SQUARE

def half_angle_polys():
    nodes = np.cos((2 * np.arange(64) + 1) * np.pi / 128)
    top = 3.15**2
    u = (nodes + 1) / 2 * top
    x = np.sqrt(u)
    fit = np.polynomial.chebyshev.Chebyshev.fit
    power = np.polynomial.Polynomial
    sine = fit(u, np.sin(x / 2) / x, 5, domain=[0, top]).convert(kind=power)
    cosine = fit(u, 2 * np.cos(x / 2), 6, domain=[0, top]).convert(kind=power)
    return [float(v) for v in sine.coef], [float(v) for v in cosine.coef]


AHEAD, LAST = 5_000_000_000, 1_500_000_000
SINE, COSINE = half_angle_polys()


def horner(coef, u):
    total = jnp.full_like(u, coef[-1])
    for c in coef[-2::-1]:
        total = total * u + c
    return total


def cos_sin(x):
    u = x * x
    s = x * horner(SINE, u)
    c2 = horner(COSINE, u)
    return 1.0 - 2.0 * (s * s), s * c2


def child_tables(degree_count):
    cheb_nodes = np.cos((2.0 * np.arange(degree_count) + 1.0) * np.pi / (2.0 * degree_count))
    lagrange = np.ones((2, degree_count, degree_count))
    for parity in range(2):
        points = (cheb_nodes + (2.0 * parity - 1.0)) / 2.0
        for target in range(degree_count):
            for source in range(degree_count):
                for others in range(degree_count):
                    if others != source:
                        lagrange[parity, target, source] *= (
                            points[target] - cheb_nodes[others]
                        ) / (cheb_nodes[source] - cheb_nodes[others])
    return lagrange


def child_blocks():
    lagrange = child_tables(P_SIZE).astype(np.float32)
    eye = np.eye(P_SIZE, dtype=np.float32)
    blocks = np.zeros((2, 2, 2, SQUARE, CH), np.float32)
    for a in range(2):
        turned = lagrange[a].T
        for slot in range(2):
            half = slice(slot * SQUARE, (slot + 1) * SQUARE)
            blocks[0, a, slot, :, half] = np.kron(turned, eye)
            blocks[1, a, slot, :, half] = np.kron(eye, turned)
    return blocks.reshape(8 * SQUARE, CH)


def expand(blocks, outs):
    for out in outs[:4]:
        out[...] = jnp.zeros_like(out)
    for axis in range(2):
        for a in range(2):
            for slot in range(2):
                part = blocks[pl.ds(((axis * 2 + a) * 2 + slot) * SQUARE, SQUARE), :]
                high = part.astype(jnp.bfloat16)
                low = (part - high.astype(jnp.float32)).astype(jnp.bfloat16)
                if axis == 1 and len(outs) > 4:
                    at = pl.ds(slot * SQUARE, SQUARE), pl.ds(a * CH, CH)
                    outs[4][at] = high
                    outs[5][at] = low
                for k in range(2):
                    rows = pl.ds(slot * CH + k * SQUARE, SQUARE)
                    columns = pl.ds((2 * a + k) * CH, CH)
                    outs[2 * axis][rows, columns] = high
                    outs[2 * axis + 1][rows, columns] = low


VMEM = pl.BlockSpec(memory_space=pltpu.VMEM)
HBM = pl.BlockSpec(memory_space=pltpu.HBM)


def limits(mib=6):
    return pltpu.CompilerParams(vmem_limit_bytes=mib * 1024 * 1024)


def load_kernel(angles, blocks, near_angles, *rest):
    sem = rest[-1]
    copy = pltpu.make_async_copy(angles, near_angles, sem)
    copy.start()
    expand(blocks, rest[:-1])
    copy.wait()


def load(angles):
    part = jax.ShapeDtypeStruct((2 * CH, 4 * CH), jnp.bfloat16)
    return pl.pallas_call(
        load_kernel,
        out_shape=[jax.ShapeDtypeStruct(angles.shape, angles.dtype)] + [part] * 4
        + [jax.ShapeDtypeStruct((CH, 2 * CH), jnp.bfloat16)] * 2,
        in_specs=[HBM, VMEM],
        out_specs=[VMEM] * 7,
        scratch_shapes=[pltpu.SemaphoreType.DMA(())],
        compiler_params=limits(),
        cost_estimate=pl.CostEstimate(
            flops=0, bytes_accessed=4 * 1024 * 1024, transcendentals=0
        ),
    )(angles, jnp.asarray(child_blocks()))


def tables_kernel(blocks, *outs):
    expand(blocks, outs)


def make_tables(blocks):
    part = jax.ShapeDtypeStruct((2 * CH, 4 * CH), jnp.bfloat16)
    return pl.pallas_call(
        tables_kernel,
        out_shape=[part] * 4,
        in_specs=[VMEM],
        out_specs=[VMEM] * 4,
        compiler_params=limits(),
        cost_estimate=pl.CostEstimate(flops=0, bytes_accessed=1024 * 1024, transcendentals=0),
    )(blocks)


def take_kernel(pick, chunks, weights, *rest):
    outs, sems = rest[:-1], rest[-1]
    t0, t3 = pick()
    copies = [
        pltpu.make_async_copy(weights.at[t0, :, t3, pl.ds(at, n), :], out, sems.at[i])
        for i, ((at, n), out) in enumerate(zip(chunks, outs))
    ]
    for copy in copies:
        copy.start()
    for copy in copies:
        copy.wait()


def take(weights, pick, chunks):
    return pl.pallas_call(
        functools.partial(take_kernel, pick, chunks),
        out_shape=[
            jax.ShapeDtypeStruct((weights.shape[1], n, CH), jnp.float32) for _, n in chunks
        ],
        in_specs=[HBM],
        out_specs=[VMEM] * len(chunks),
        scratch_shapes=[pltpu.SemaphoreType.DMA((len(chunks),))],
        compiler_params=limits(),
        cost_estimate=pl.CostEstimate(
            flops=20_000_000_000, bytes_accessed=4 * 1024 * 1024, transcendentals=0
        ),
    )(weights)


def own_bit(k):
    axis = ("gx", "gy")[k % 2]
    bit = lax.axis_size(axis).bit_length() - 2 - k // 2
    return lax.axis_index(axis) >> bit & 1


def turn(y, angle):
    c, s = cos_sin(angle)
    re, im = y[:, :CH], y[:, CH:]
    u = c * re - s * im
    v = s * re + c * im
    left = lax.broadcasted_iota(jnp.int32, u.shape, 1) < SQUARE
    return jnp.where(left, u, v) + pltpu.roll(jnp.where(left, v, u), SQUARE, 1)


def level_kernel(level, segments, tile, own, arr, ang, high, low, out, scratch):
    upper = own_bit(level) == 1

    def piece(parts):
        count = sum(n for *_, n in parts)
        near, far = (
            jnp.concatenate([ref[pl.ds(row[k], row[4]), :] for row in parts], axis=0)
            for k, ref in ((0, own), (1, arr))
        )
        x = jnp.concatenate([jnp.where(upper, far, near), jnp.where(upper, near, far)], axis=1)
        x_hi = x.astype(jnp.bfloat16)
        x_lo = (x - x_hi.astype(jnp.float32)).astype(jnp.bfloat16)
        dot = functools.partial(jnp.dot, preferred_element_type=jnp.float32)
        y = dot(x_hi, high[...]) + (dot(x_lo, high[...]) + dot(x_hi, low[...]))
        at = 0
        for _, _, row, _, n in parts:
            scratch[pl.ds(2 * at, 2 * n), :] = ang[pl.ds(row, 2 * n), :].astype(jnp.float32)
            at += n
        for a in range(2):
            turned = turn(
                y[:, 2 * a * CH : 2 * (a + 1) * CH], scratch[pl.ds(a, count, stride=2), :]
            )
            at = 0
            for _, _, _, row, n in parts:
                out[pl.ds(row + a, n, stride=2), :] = turned[at : at + n]
                at += n

    parts = segments()
    if len(parts) > 1 or parts[0][4] == tile:
        piece(parts)
        return

    for row_own, row_arr, row_ang, row_out, n in parts:

        def step(i):
            b = pl.multiple_of(i * tile, tile)
            piece([(row_own + b, row_arr + b, row_ang + 2 * b, row_out + 2 * b, tile)])

        pl.loop(0, n // tile)(step)


def level_call(level, segments, own, arr, ang, table, rows, weight=0):
    steps = -(-rows // 512)
    tile = rows // 2 // steps
    kernel = functools.partial(level_kernel, level, segments, tile)
    scratch = [pltpu.VMEM((2 * tile, CH), jnp.float32)]
    return pl.pallas_call(
        kernel,
        out_shape=jax.ShapeDtypeStruct((rows, CH), jnp.float32),
        in_specs=[VMEM] * 5,
        out_specs=VMEM,
        scratch_shapes=scratch,
        compiler_params=limits(),
        cost_estimate=pl.CostEstimate(
            flops=weight, bytes_accessed=rows * 8 * 1024, transcendentals=0
        ),
    )(own, arr, ang, *table)


def fetch_kernel(row, far, near, sem):
    copy = pltpu.make_async_copy(far.at[pl.ds(row, near.shape[0])], near, sem)
    copy.start()
    copy.wait()


def fetch(far, row, rows):
    return pl.pallas_call(
        functools.partial(fetch_kernel, row),
        out_shape=jax.ShapeDtypeStruct((rows, CH), far.dtype),
        in_specs=[pl.BlockSpec(memory_space=pl.ANY)],
        out_specs=VMEM,
        scratch_shapes=[pltpu.SemaphoreType.DMA(())],
        compiler_params=limits(),
        cost_estimate=pl.CostEstimate(flops=0, bytes_accessed=1024 * 1024, transcendentals=0),
    )(far)


def direct_kernel(row, own, arr, ang, high, low, *rest):
    out, scratch, near_out, sems = rest[-4:]
    count, rows = near_out.shape[:2]
    tile = rows // 2
    copies = []
    for i in range(count):
        at = i * tile
        part = near_out.at[i]
        segment = (row + at, at, 2 * (row + at), 0, tile)
        level_kernel(3, lambda: [segment], tile, own, arr, ang, high, low, part, scratch)
        copy = pltpu.make_async_copy(
            part, out.at[pl.ds(2 * (row + at), rows)], sems.at[i]
        )
        copy.start()
        copies.append(copy)
    for copy in copies:
        copy.wait()


def direct_call(own, arr, ang, table, row, boxes):
    rows = arr.shape[0]
    count = -(-rows // 256)
    tile = rows // count
    return pl.pallas_call(
        functools.partial(direct_kernel, row),
        out_shape=jax.ShapeDtypeStruct((boxes, CH), jnp.float32),
        in_specs=[VMEM] * 5,
        out_specs=HBM,
        scratch_shapes=[
            pltpu.VMEM((2 * tile, CH), jnp.float32),
            pltpu.VMEM((count, 2 * tile, CH), jnp.float32),
            pltpu.SemaphoreType.DMA((count,)),
        ],
        compiler_params=limits(),
        cost_estimate=pl.CostEstimate(
            flops=LAST, bytes_accessed=rows * 8 * 1024, transcendentals=0
        ),
    )(own, arr, ang, *table)


def tile_of(rows):
    return next(n for n in (128, 144, 112, 96) if rows % n == 0)


def spread_last(x, high, low, scratch):
    n = x.shape[0]
    x_hi = x.astype(jnp.bfloat16)
    x_lo = (x - x_hi.astype(jnp.float32)).astype(jnp.bfloat16)
    dot = functools.partial(jnp.dot, preferred_element_type=jnp.float32)
    y = dot(x_hi, high[...]) + (dot(x_lo, high[...]) + dot(x_hi, low[...]))
    for a in range(2):
        scratch[pl.ds(a, n, stride=2), :] = y[:, a * CH : (a + 1) * CH]
    return scratch[...]


def before_kernel(row, tile, own, ang, high, low, part, cos_out, sin_out, scratch):
    upper = own_bit(3) == 1

    def step(i):
        rows = pl.ds(pl.multiple_of(2 * i * tile, 2 * tile), 2 * tile)
        near = pl.ds(pl.multiple_of(row + i * tile, 16), tile)
        y = spread_last(own[near, :], high, low, scratch)
        at = pl.ds(pl.multiple_of(2 * (row + i * tile), 32), 2 * tile)
        c, s = cos_sin(ang[at, :].astype(jnp.float32))
        left = lax.broadcasted_iota(jnp.int32, c.shape, 1) < SQUARE
        c_far, s_far = pltpu.roll(c, SQUARE, 1), pltpu.roll(s, SQUARE, 1)
        c0, c1 = jnp.where(left, c, c_far), jnp.where(left, c_far, c)
        s0, s1 = jnp.where(left, -s, s_far), jnp.where(left, -s_far, s)
        part[rows, :] = jnp.where(upper, c1, c0) * y + jnp.where(upper, s1, s0) * pltpu.roll(
            y, SQUARE, 1
        )
        cos_out[rows, :] = jnp.where(upper, c0, c1)
        sin_out[rows, :] = jnp.where(upper, s0, s1)

    pl.loop(0, part.shape[0] // (2 * tile))(step)


def before_call(own, ang, table, row):
    tile = tile_of(own.shape[0] - row)
    part = jax.ShapeDtypeStruct((2 * (own.shape[0] - row), CH), jnp.float32)
    return pl.pallas_call(
        functools.partial(before_kernel, row, tile),
        out_shape=[part] * 3,
        in_specs=[VMEM] * 4,
        out_specs=[VMEM] * 3,
        scratch_shapes=[pltpu.VMEM((2 * tile, CH), jnp.float32)],
        compiler_params=limits(),
        cost_estimate=pl.CostEstimate(
            flops=0, bytes_accessed=4 * 1024 * 1024, transcendentals=0
        ),
    )(own, ang, *table)


def last_kernel(row, arr, part, cos_in, sin_in, high, low, *rest):
    out, scratch, near_out, sems = rest[-4:]
    count, rows = near_out.shape[:2]
    tile = rows // 2
    copies = []
    for i in range(count):
        at = pl.ds(i * rows, rows)
        y = spread_last(arr[pl.ds(i * tile, tile), :], high, low, scratch.at[i])
        near_out[i] = (
            part[at, :] + cos_in[at, :] * y + sin_in[at, :] * pltpu.roll(y, SQUARE, 1)
        )
        copy = pltpu.make_async_copy(
            near_out.at[i], out.at[pl.ds(2 * row + i * rows, rows)], sems.at[i]
        )
        copy.start()
        copies.append(copy)
    for copy in copies:
        copy.wait()


def last_call(arr, ready, table, row, earlier):
    rows = arr.shape[0]
    tile = tile_of(rows)
    count = rows // tile
    operands = [arr, *ready, *table, earlier]
    return pl.pallas_call(
        functools.partial(last_kernel, row),
        out_shape=jax.ShapeDtypeStruct(earlier.shape, jnp.float32),
        in_specs=[VMEM] * 6 + [HBM],
        out_specs=HBM,
        scratch_shapes=[
            pltpu.VMEM((count, 2 * tile, CH), jnp.float32),
            pltpu.VMEM((count, 2 * tile, CH), jnp.float32),
            pltpu.SemaphoreType.DMA((count,)),
        ],
        input_output_aliases={6: 0},
        compiler_params=limits(),
        cost_estimate=pl.CostEstimate(
            flops=0, bytes_accessed=rows * 8 * 1024, transcendentals=0
        ),
    )(*operands)


def from_partner(block, axis, bit):
    count = lax.axis_size(axis)
    route = [(low, low ^ (1 << bit)) for low in range(count)]
    return lax.ppermute(block, axis, route)


def after(value, *others):
    return lax.optimization_barrier((value, *others))[0]


def shards(weights, angles):
    bits_x = lax.axis_size("gx").bit_length() - 1
    bits_y = lax.axis_size("gy").bit_length() - 1
    boxes = weights.shape[2]
    base = boxes // 16
    far = weights.reshape(boxes, CH)
    w2 = far
    env = [None] * 4
    ang_far = angles.reshape(4 * boxes, CH)
    aligned = lambda row, by=16: pl.multiple_of(row, by)

    def target(k, other):
        return 1 - own_bit(k) if other else own_bit(k)

    def first(chunks, given):
        def pick():
            return 1 - own_bit(0), target(3, given)

        return [
            part.reshape(-1, CH) for part in take(far.reshape(2, 4, 2, base, CH), pick, chunks)
        ]

    def swap0(part):
        return from_partner(part, "gx", bits_x - 1)

    def level0(chunk, given, arr, send, weight=0):
        at, n = chunk

        def segments():
            t1, t3 = target(1, send), target(3, given)
            parts = []
            for t2 in range(2):
                low = (t1 * 2 + t2) * 2 + t3
                parts.append(
                    (
                        aligned((own_bit(0) * 8 + low) * base + at, 8),
                        aligned((t1 * 2 + t2) * n, 8),
                        aligned(low * 2 * base + 2 * at),
                        t2 * 2 * n,
                        n,
                    )
                )
            return parts

        return level_call(0, segments, env[3], arr, env[0], env[1], 4 * n, weight)

    def level1(chunk, given, own, arr, send, weight=0):
        at, n = chunk

        def segments():
            t2, t3 = target(2, send), target(3, given)
            row = aligned(t2 * 2 * n)
            return [(row, row, aligned(boxes + (t2 * 2 + t3) * 4 * base + 4 * at), 0, 2 * n)]

        return level_call(1, segments, own, arr, env[0], env[2], 4 * n, weight)

    def level2(chunk, given, own, arr):
        at, n = chunk

        def segments():
            t3 = target(3, given)
            return [(0, 0, aligned(2 * boxes + t3 * 8 * base + 8 * at), 0, 4 * n)]

        return level_call(2, segments, own, arr, env[0], env[1], 8 * n)

    def swap1(part):
        return from_partner(part, "gy", bits_y - 1)

    def swap2(part):
        return from_partner(part, "gx", bits_x - 2)

    def swap3(part):
        return from_partner(part, "gy", bits_y - 2)

    cut = 7 * base // 16
    a, b, k = (0, cut), (cut, base - cut), (0, base)
    send_a, send_b = first([a, b], True)
    arr_a, arr_b = swap0(send_a), swap0(send_b)
    ang, *ready = load(after(ang_far, send_a))
    tab_x, tab_y, tab_last = ready[:2], ready[2:4], ready[4:]
    env[:] = [ang, tab_x, tab_y, after(w2, send_b)]
    send_a = level0(a, True, arr_a, True, AHEAD)
    arr1_a = swap1(send_a)
    keep_a = level0(a, True, after(arr_a, send_a), False, AHEAD)
    send_b = level0(b, True, after(arr_b, keep_a), True)
    arr1_b = swap1(send_b)
    send_a = level1(a, True, keep_a, after(arr1_a, send_b), True, AHEAD)
    arr2_a = swap2(send_a)
    keep_b = level0(b, True, after(arr_b, send_a), False)
    send_b = level1(b, True, keep_b, arr1_b, True)
    arr2_b = swap2(send_b)
    keep_a = level1(a, True, keep_a, arr1_a, False)
    given_a = level2(a, True, keep_a, after(arr2_a, send_b))
    z_a = swap3(given_a)

    keep_b = level1(b, True, keep_b, after(arr1_b, given_a), False)
    given_b = level2(b, True, keep_b, arr2_b)
    z_b = swap3(given_b)

    here = after(lax.axis_index("gx"), given_b[0, 0]) < lax.axis_size("gx")

    def beside(w2, ang, blocks):
        nonlocal far
        far = w2
        ready = make_tables(blocks)
        env[:] = [ang, ready[:2], ready[2:], w2]
        arr_k = swap0(first([k], False)[0])
        arr1_k = swap1(level0(k, False, arr_k, True))
        keep_k = level0(k, False, arr_k, False)
        arr2_k = swap2(level1(k, False, keep_k, arr1_k, True))
        keep_k = level1(k, False, keep_k, arr1_k, False)
        return level2(k, False, keep_k, arr2_k)

    kept = lax.cond(
        here, beside, lambda *_: jnp.zeros((8 * base, CH)), far, ang_far, jnp.asarray(child_blocks())
    )
    near_ang = fetch(after(ang_far, kept), 3 * boxes, boxes)
    kept = after(kept, near_ang)
    done = before_call(kept, near_ang, tab_last, 8 * cut)
    out = direct_call(after(kept, done[0]), z_a, near_ang, tab_y, 0, boxes)
    out = last_call(z_b, done, tab_last, 8 * cut, out)
    return out.reshape(1, 1, boxes, CH)


def solution(mesh):
    return jax.shard_map(
        shards,
        mesh=mesh,
        in_specs=(P("gx", "gy", None, None), P(None, "gx", "gy", None, None)),
        out_specs=P("gx", "gy", None, None),
        check_vma=False,
    )
```

```python
import functools

import jax
import jax.numpy as jnp
import ml_dtypes
import numpy as np
from jax import lax
from jax.experimental import pallas as pl
from jax.experimental.pallas import tpu as pltpu
from jax.sharding import PartitionSpec as P

P_SIZE = 8
SQUARE = P_SIZE * P_SIZE
CH = 2 * SQUARE

def half_angle_polys():
    nodes = np.cos((2 * np.arange(64) + 1) * np.pi / 128)
    top = 3.15**2
    u = (nodes + 1) / 2 * top
    x = np.sqrt(u)
    fit = np.polynomial.chebyshev.Chebyshev.fit
    power = np.polynomial.Polynomial
    sine = fit(u, np.sin(x / 2) / x, 5, domain=[0, top]).convert(kind=power)
    cosine = fit(u, 2 * np.cos(x / 2), 6, domain=[0, top]).convert(kind=power)
    return [float(v) for v in sine.coef], [float(v) for v in cosine.coef]


AHEAD, LAST = 5_000_000_000, 1_500_000_000
SINE, COSINE = half_angle_polys()


def horner(coef, u):
    total = jnp.full_like(u, coef[-1])
    for c in coef[-2::-1]:
        total = total * u + c
    return total


def cos_sin(x):
    u = x * x
    s = x * horner(SINE, u)
    c2 = horner(COSINE, u)
    return 1.0 - 2.0 * (s * s), s * c2


def child_tables(degree_count):
    cheb_nodes = np.cos((2.0 * np.arange(degree_count) + 1.0) * np.pi / (2.0 * degree_count))
    lagrange = np.ones((2, degree_count, degree_count))
    for parity in range(2):
        points = (cheb_nodes + (2.0 * parity - 1.0)) / 2.0
        for target in range(degree_count):
            for source in range(degree_count):
                for others in range(degree_count):
                    if others != source:
                        lagrange[parity, target, source] *= (
                            points[target] - cheb_nodes[others]
                        ) / (cheb_nodes[source] - cheb_nodes[others])
    return lagrange


def child_blocks():
    lagrange = child_tables(P_SIZE).astype(np.float32)
    eye = np.eye(P_SIZE, dtype=np.float32)
    blocks = np.zeros((2, 2, 2, SQUARE, CH), np.float32)
    for a in range(2):
        turned = lagrange[a].T
        for slot in range(2):
            half = slice(slot * SQUARE, (slot + 1) * SQUARE)
            blocks[0, a, slot, :, half] = np.kron(turned, eye)
            blocks[1, a, slot, :, half] = np.kron(eye, turned)
    return blocks.reshape(8 * SQUARE, CH)


def expand(blocks, outs):
    for out in outs[:4]:
        out[...] = jnp.zeros_like(out)
    for axis in range(2):
        for a in range(2):
            for slot in range(2):
                part = blocks[pl.ds(((axis * 2 + a) * 2 + slot) * SQUARE, SQUARE), :]
                high = part.astype(jnp.bfloat16)
                low = (part - high.astype(jnp.float32)).astype(jnp.bfloat16)
                if axis == 1 and len(outs) > 4:
                    at = pl.ds(slot * SQUARE, SQUARE), pl.ds(a * CH, CH)
                    outs[4][at] = high
                    outs[5][at] = low
                for k in range(2):
                    rows = pl.ds(slot * CH + k * SQUARE, SQUARE)
                    columns = pl.ds((2 * a + k) * CH, CH)
                    outs[2 * axis][rows, columns] = high
                    outs[2 * axis + 1][rows, columns] = low


VMEM = pl.BlockSpec(memory_space=pltpu.VMEM)
HBM = pl.BlockSpec(memory_space=pltpu.HBM)


def limits(mib=6):
    return pltpu.CompilerParams(vmem_limit_bytes=mib * 1024 * 1024)


def load_kernel(angles, blocks, near_angles, *rest):
    sem = rest[-1]
    copy = pltpu.make_async_copy(angles, near_angles, sem)
    copy.start()
    expand(blocks, rest[:-1])
    copy.wait()


def load(angles):
    part = jax.ShapeDtypeStruct((2 * CH, 4 * CH), jnp.bfloat16)
    return pl.pallas_call(
        load_kernel,
        out_shape=[jax.ShapeDtypeStruct(angles.shape, angles.dtype)] + [part] * 4
        + [jax.ShapeDtypeStruct((CH, 2 * CH), jnp.bfloat16)] * 2,
        in_specs=[HBM, VMEM],
        out_specs=[VMEM] * 7,
        scratch_shapes=[pltpu.SemaphoreType.DMA(())],
        compiler_params=limits(),
        cost_estimate=pl.CostEstimate(
            flops=0, bytes_accessed=4 * 1024 * 1024, transcendentals=0
        ),
    )(angles, jnp.asarray(child_blocks()))


def tables_kernel(blocks, *outs):
    expand(blocks, outs)


def make_tables(blocks):
    part = jax.ShapeDtypeStruct((2 * CH, 4 * CH), jnp.bfloat16)
    return pl.pallas_call(
        tables_kernel,
        out_shape=[part] * 4,
        in_specs=[VMEM],
        out_specs=[VMEM] * 4,
        compiler_params=limits(),
        cost_estimate=pl.CostEstimate(flops=0, bytes_accessed=1024 * 1024, transcendentals=0),
    )(blocks)


def take_kernel(pick, chunks, weights, *rest):
    outs, sems = rest[:-1], rest[-1]
    t0, t3 = pick()
    copies = [
        pltpu.make_async_copy(weights.at[t0, :, t3, pl.ds(at, n), :], out, sems.at[i])
        for i, ((at, n), out) in enumerate(zip(chunks, outs))
    ]
    for copy in copies:
        copy.start()
    for copy in copies:
        copy.wait()


def take(weights, pick, chunks):
    return pl.pallas_call(
        functools.partial(take_kernel, pick, chunks),
        out_shape=[
            jax.ShapeDtypeStruct((weights.shape[1], n, CH), jnp.float32) for _, n in chunks
        ],
        in_specs=[HBM],
        out_specs=[VMEM] * len(chunks),
        scratch_shapes=[pltpu.SemaphoreType.DMA((len(chunks),))],
        compiler_params=limits(),
        cost_estimate=pl.CostEstimate(
            flops=20_000_000_000, bytes_accessed=4 * 1024 * 1024, transcendentals=0
        ),
    )(weights)


def own_bit(k):
    axis = ("gx", "gy")[k % 2]
    bit = lax.axis_size(axis).bit_length() - 2 - k // 2
    return lax.axis_index(axis) >> bit & 1


def turn(y, angle):
    c, s = cos_sin(angle)
    re, im = y[:, :CH], y[:, CH:]
    u = c * re - s * im
    v = s * re + c * im
    left = lax.broadcasted_iota(jnp.int32, u.shape, 1) < SQUARE
    return jnp.where(left, u, v) + pltpu.roll(jnp.where(left, v, u), SQUARE, 1)


def level_kernel(level, segments, tile, own, arr, ang, high, low, out, scratch):
    upper = own_bit(level) == 1

    def piece(parts):
        count = sum(n for *_, n in parts)
        near, far = (
            jnp.concatenate([ref[pl.ds(row[k], row[4]), :] for row in parts], axis=0)
            for k, ref in ((0, own), (1, arr))
        )
        x = jnp.concatenate([jnp.where(upper, far, near), jnp.where(upper, near, far)], axis=1)
        x_hi = x.astype(jnp.bfloat16)
        x_lo = (x - x_hi.astype(jnp.float32)).astype(jnp.bfloat16)
        dot = functools.partial(jnp.dot, preferred_element_type=jnp.float32)
        y = dot(x_hi, high[...]) + (dot(x_lo, high[...]) + dot(x_hi, low[...]))
        at = 0
        for _, _, row, _, n in parts:
            scratch[pl.ds(2 * at, 2 * n), :] = ang[pl.ds(row, 2 * n), :].astype(jnp.float32)
            at += n
        for a in range(2):
            turned = turn(
                y[:, 2 * a * CH : 2 * (a + 1) * CH], scratch[pl.ds(a, count, stride=2), :]
            )
            at = 0
            for _, _, _, row, n in parts:
                out[pl.ds(row + a, n, stride=2), :] = turned[at : at + n]
                at += n

    parts = segments()
    if len(parts) > 1 or parts[0][4] == tile:
        piece(parts)
        return

    for row_own, row_arr, row_ang, row_out, n in parts:

        def step(i):
            b = pl.multiple_of(i * tile, tile)
            piece([(row_own + b, row_arr + b, row_ang + 2 * b, row_out + 2 * b, tile)])

        pl.loop(0, n // tile)(step)


def level_call(level, segments, own, arr, ang, table, rows, weight=0):
    steps = -(-rows // 512)
    tile = rows // 2 // steps
    kernel = functools.partial(level_kernel, level, segments, tile)
    scratch = [pltpu.VMEM((2 * tile, CH), jnp.float32)]
    return pl.pallas_call(
        kernel,
        out_shape=jax.ShapeDtypeStruct((rows, CH), jnp.float32),
        in_specs=[VMEM] * 5,
        out_specs=VMEM,
        scratch_shapes=scratch,
        compiler_params=limits(),
        cost_estimate=pl.CostEstimate(
            flops=weight, bytes_accessed=rows * 8 * 1024, transcendentals=0
        ),
    )(own, arr, ang, *table)


def fetch_kernel(row, far, near, sem):
    copy = pltpu.make_async_copy(far.at[pl.ds(row, near.shape[0])], near, sem)
    copy.start()
    copy.wait()


def fetch(far, row, rows):
    return pl.pallas_call(
        functools.partial(fetch_kernel, row),
        out_shape=jax.ShapeDtypeStruct((rows, CH), far.dtype),
        in_specs=[pl.BlockSpec(memory_space=pl.ANY)],
        out_specs=VMEM,
        scratch_shapes=[pltpu.SemaphoreType.DMA(())],
        compiler_params=limits(),
        cost_estimate=pl.CostEstimate(flops=0, bytes_accessed=1024 * 1024, transcendentals=0),
    )(far)


def direct_kernel(row, own, arr, ang, high, low, *rest):
    out, scratch, near_out, sems = rest[-4:]
    count, rows = near_out.shape[:2]
    tile = rows // 2
    copies = []
    for i in range(count):
        at = i * tile
        part = near_out.at[i]
        segment = (row + at, at, 2 * (row + at), 0, tile)
        level_kernel(3, lambda: [segment], tile, own, arr, ang, high, low, part, scratch)
        copy = pltpu.make_async_copy(
            part, out.at[pl.ds(2 * (row + at), rows)], sems.at[i]
        )
        copy.start()
        copies.append(copy)
    for copy in copies:
        copy.wait()


def direct_call(own, arr, ang, table, row, boxes):
    rows = arr.shape[0]
    count = -(-rows // 256)
    tile = rows // count
    return pl.pallas_call(
        functools.partial(direct_kernel, row),
        out_shape=jax.ShapeDtypeStruct((boxes, CH), jnp.float32),
        in_specs=[VMEM] * 5,
        out_specs=HBM,
        scratch_shapes=[
            pltpu.VMEM((2 * tile, CH), jnp.float32),
            pltpu.VMEM((count, 2 * tile, CH), jnp.float32),
            pltpu.SemaphoreType.DMA((count,)),
        ],
        compiler_params=limits(),
        cost_estimate=pl.CostEstimate(
            flops=LAST, bytes_accessed=rows * 8 * 1024, transcendentals=0
        ),
    )(own, arr, ang, *table)


def tile_of(rows):
    return next(n for n in (128, 144, 112, 96) if rows % n == 0)


def spread_last(x, high, low, scratch):
    n = x.shape[0]
    x_hi = x.astype(jnp.bfloat16)
    x_lo = (x - x_hi.astype(jnp.float32)).astype(jnp.bfloat16)
    dot = functools.partial(jnp.dot, preferred_element_type=jnp.float32)
    y = dot(x_hi, high[...]) + (dot(x_lo, high[...]) + dot(x_hi, low[...]))
    for a in range(2):
        scratch[pl.ds(a, n, stride=2), :] = y[:, a * CH : (a + 1) * CH]
    return scratch[...]


def before_kernel(row, tile, own, ang, high, low, part, cos_out, sin_out, scratch):
    upper = own_bit(3) == 1

    def step(i):
        rows = pl.ds(pl.multiple_of(2 * i * tile, 2 * tile), 2 * tile)
        near = pl.ds(pl.multiple_of(row + i * tile, 16), tile)
        y = spread_last(own[near, :], high, low, scratch)
        at = pl.ds(pl.multiple_of(2 * (row + i * tile), 32), 2 * tile)
        c, s = cos_sin(ang[at, :].astype(jnp.float32))
        left = lax.broadcasted_iota(jnp.int32, c.shape, 1) < SQUARE
        c_far, s_far = pltpu.roll(c, SQUARE, 1), pltpu.roll(s, SQUARE, 1)
        c0, c1 = jnp.where(left, c, c_far), jnp.where(left, c_far, c)
        s0, s1 = jnp.where(left, -s, s_far), jnp.where(left, -s_far, s)
        part[rows, :] = jnp.where(upper, c1, c0) * y + jnp.where(upper, s1, s0) * pltpu.roll(
            y, SQUARE, 1
        )
        cos_out[rows, :] = jnp.where(upper, c0, c1)
        sin_out[rows, :] = jnp.where(upper, s0, s1)

    pl.loop(0, part.shape[0] // (2 * tile))(step)


def before_call(own, ang, table, row):
    tile = tile_of(own.shape[0] - row)
    part = jax.ShapeDtypeStruct((2 * (own.shape[0] - row), CH), jnp.float32)
    return pl.pallas_call(
        functools.partial(before_kernel, row, tile),
        out_shape=[part] * 3,
        in_specs=[VMEM] * 4,
        out_specs=[VMEM] * 3,
        scratch_shapes=[pltpu.VMEM((2 * tile, CH), jnp.float32)],
        compiler_params=limits(),
        cost_estimate=pl.CostEstimate(
            flops=0, bytes_accessed=4 * 1024 * 1024, transcendentals=0
        ),
    )(own, ang, *table)


def last_kernel(row, arr, part, cos_in, sin_in, high, low, *rest):
    out, scratch, near_out, sems = rest[-4:]
    count, rows = near_out.shape[:2]
    tile = rows // 2
    copies = []
    for i in range(count):
        at = pl.ds(i * rows, rows)
        y = spread_last(arr[pl.ds(i * tile, tile), :], high, low, scratch.at[i])
        near_out[i] = (
            part[at, :] + cos_in[at, :] * y + sin_in[at, :] * pltpu.roll(y, SQUARE, 1)
        )
        copy = pltpu.make_async_copy(
            near_out.at[i], out.at[pl.ds(2 * row + i * rows, rows)], sems.at[i]
        )
        copy.start()
        copies.append(copy)
    for copy in copies:
        copy.wait()


def last_call(arr, ready, table, row, earlier):
    rows = arr.shape[0]
    tile = 96 if rows % 96 == 0 else tile_of(rows)
    count = rows // tile
    operands = [arr, *ready, *table, earlier]
    return pl.pallas_call(
        functools.partial(last_kernel, row),
        out_shape=jax.ShapeDtypeStruct(earlier.shape, jnp.float32),
        in_specs=[VMEM] * 6 + [HBM],
        out_specs=HBM,
        scratch_shapes=[
            pltpu.VMEM((count, 2 * tile, CH), jnp.float32),
            pltpu.VMEM((count, 2 * tile, CH), jnp.float32),
            pltpu.SemaphoreType.DMA((count,)),
        ],
        input_output_aliases={6: 0},
        compiler_params=limits(),
        cost_estimate=pl.CostEstimate(
            flops=0, bytes_accessed=rows * 8 * 1024, transcendentals=0
        ),
    )(*operands)


def from_partner(block, axis, bit):
    count = lax.axis_size(axis)
    route = [(low, low ^ (1 << bit)) for low in range(count)]
    return lax.ppermute(block, axis, route)


def after(value, *others):
    return lax.optimization_barrier((value, *others))[0]


def shards(weights, angles):
    bits_x = lax.axis_size("gx").bit_length() - 1
    bits_y = lax.axis_size("gy").bit_length() - 1
    boxes = weights.shape[2]
    base = boxes // 16
    far = weights.reshape(boxes, CH)
    w2 = far
    env = [None] * 4
    ang_far = angles.reshape(4 * boxes, CH)
    aligned = lambda row, by=16: pl.multiple_of(row, by)

    def target(k, other):
        return 1 - own_bit(k) if other else own_bit(k)

    def first(chunks, given):
        def pick():
            return 1 - own_bit(0), target(3, given)

        return [
            part.reshape(-1, CH) for part in take(far.reshape(2, 4, 2, base, CH), pick, chunks)
        ]

    def swap0(part):
        return from_partner(part, "gx", bits_x - 1)

    def level0(chunk, given, arr, send, weight=0):
        at, n = chunk

        def segments():
            t1, t3 = target(1, send), target(3, given)
            parts = []
            for t2 in range(2):
                low = (t1 * 2 + t2) * 2 + t3
                parts.append(
                    (
                        aligned((own_bit(0) * 8 + low) * base + at, 8),
                        aligned((t1 * 2 + t2) * n, 8),
                        aligned(low * 2 * base + 2 * at),
                        t2 * 2 * n,
                        n,
                    )
                )
            return parts

        return level_call(0, segments, env[3], arr, env[0], env[1], 4 * n, weight)

    def level1(chunk, given, own, arr, send, weight=0):
        at, n = chunk

        def segments():
            t2, t3 = target(2, send), target(3, given)
            row = aligned(t2 * 2 * n)
            return [(row, row, aligned(boxes + (t2 * 2 + t3) * 4 * base + 4 * at), 0, 2 * n)]

        return level_call(1, segments, own, arr, env[0], env[2], 4 * n, weight)

    def level2(chunk, given, own, arr):
        at, n = chunk

        def segments():
            t3 = target(3, given)
            return [(0, 0, aligned(2 * boxes + t3 * 8 * base + 8 * at), 0, 4 * n)]

        return level_call(2, segments, own, arr, env[0], env[1], 8 * n)

    def swap1(part):
        return from_partner(part, "gy", bits_y - 1)

    def swap2(part):
        return from_partner(part, "gx", bits_x - 2)

    def swap3(part):
        return from_partner(part, "gy", bits_y - 2)

    cut = 7 * base // 16
    a, b, k = (0, cut), (cut, base - cut), (0, base)
    send_a, send_b = first([a, b], True)
    arr_a, arr_b = swap0(send_a), swap0(send_b)
    ang, *ready = load(after(ang_far, send_a))
    tab_x, tab_y, tab_last = ready[:2], ready[2:4], ready[4:]
    env[:] = [ang, tab_x, tab_y, after(w2, send_b)]
    send_a = level0(a, True, arr_a, True, AHEAD)
    arr1_a = swap1(send_a)
    keep_a = level0(a, True, after(arr_a, send_a), False, AHEAD)
    send_b = level0(b, True, after(arr_b, keep_a), True)
    arr1_b = swap1(send_b)
    send_a = level1(a, True, keep_a, after(arr1_a, send_b), True, AHEAD)
    arr2_a = swap2(send_a)
    keep_b = level0(b, True, after(arr_b, send_a), False)
    send_b = level1(b, True, keep_b, arr1_b, True)
    arr2_b = swap2(send_b)
    keep_a = level1(a, True, keep_a, arr1_a, False)
    given_a = level2(a, True, keep_a, after(arr2_a, send_b))
    z_a = swap3(given_a)

    keep_b = level1(b, True, keep_b, after(arr1_b, given_a), False)
    given_b = level2(b, True, keep_b, arr2_b)
    z_b = swap3(given_b)

    here = after(lax.axis_index("gx"), given_b[0, 0]) < lax.axis_size("gx")

    def beside(w2, ang, blocks):
        nonlocal far
        far = w2
        ready = make_tables(blocks)
        env[:] = [ang, ready[:2], ready[2:], w2]
        arr_k = swap0(first([k], False)[0])
        arr1_k = swap1(level0(k, False, arr_k, True))
        keep_k = level0(k, False, arr_k, False)
        arr2_k = swap2(level1(k, False, keep_k, arr1_k, True))
        keep_k = level1(k, False, keep_k, arr1_k, False)
        return level2(k, False, keep_k, arr2_k)

    kept = lax.cond(
        here, beside, lambda *_: jnp.zeros((8 * base, CH)), far, ang_far, jnp.asarray(child_blocks())
    )
    near_ang = fetch(after(ang_far, kept), 3 * boxes, boxes)
    kept = after(kept, near_ang)
    done = before_call(kept, near_ang, tab_last, 8 * cut)
    out = direct_call(after(kept, done[0]), z_a, near_ang, tab_y, 0, boxes)
    out = last_call(z_b, done, tab_last, 8 * cut, out)
    return out.reshape(1, 1, boxes, CH)


def solution(mesh):
    return jax.shard_map(
        shards,
        mesh=mesh,
        in_specs=(P("gx", "gy", None, None), P(None, "gx", "gy", None, None)),
        out_specs=P("gx", "gy", None, None),
        check_vma=False,
    )
```
